256 devices in a mesh: row: 16 (over z, y_hi), col: 16 (over x, y_lo, core).
Axes of the slice: x: 4, y: 4 (y_hi: 2, y_lo: 2; y = y_hi * 2 + y_lo), z: 8, core: 2. Of those that a mesh axis runs over, the one named last changes fastest.
Arguments:
- grad_out: bfloat16 [16, 4096, 1024], P('row', 'col'), may hold values from -6 to 6
- preact: bfloat16 [16, 4096, 1024], P('row', 'col'), may hold values from -8 to 8
- features: bfloat16 [16, 4096, 1024], P('col', 'row'), may hold values from -6 to 6
- weight: bfloat16 [1024, 1024], replicated, may hold values from -0.1875 to 0.1875
- tile_values: bfloat16 [16, 16, 80, 128, 128], P('row', 'col'), may hold values from -0.125 to 0.125
- tile_row: int32 [16, 16, 80], P('row', 'col'), may hold values from 0 to 31, as said below
- tile_col: int32 [16, 16, 80], P('row', 'col'), may hold values from 0 to 31
- tile_count: int32 [16, 16], P('row', 'col'), may hold values from 1 to 80, as said below
Outputs:
- grad_in: bfloat16 [16, 4096, 1024], P('col', 'row')
- grad_weight: float32 [1024, 1024], replicated
The draws below stay inside these ranges and needn't reach their ends.
Inputs may be any that keep to these rules, and one draw needn't show every extreme that they name: `tile_count`: some block uses all 80 slots. Within a block, the slots below its count name distinct (tile_row, tile_col) pairs; the other slots are ignored.
All inputs are finite; a program needn't handle non-finite values.
Results may differ from the reference program's by a relative error of at most 0.023.
Values may be sent and summed in bfloat16 or wider, within the bound.
No kernel may reach another device: no remote copies, remote signals or barrier semaphores. Data moves between devices by JAX's collectives and lax.ppermute only.
A program may use at most 128 MiB of HBM per device.

```python
import jax
import jax.numpy as jnp
from jax import lax

F = 1024
TILE = 128
PROW = 16
PCOL = 16
ROW_TILES = 32
COL_TILES = 32
K_MAX = 80
N_ROW = 16


def tile_slots(key):
    device_keys = jax.random.split(key, PROW * PCOL)

    def device_slots(sub_key):
        return jax.random.permutation(sub_key, ROW_TILES * COL_TILES)[:K_MAX]
    return jax.vmap(device_slots)(device_keys).reshape(PROW, PCOL, K_MAX).astype(jnp.int32)


def draw_tile_row(key, part):
    slots_drawn = tile_slots(key)
    return (slots_drawn // COL_TILES).astype(jnp.int32)


def draw_tile_col(key, part):
    slots_drawn = tile_slots(key)
    return (slots_drawn % COL_TILES).astype(jnp.int32)


def draw_tile_count(key, part):
    key = jax.random.fold_in(key, 7)
    key_count, key_pick = jax.random.split(key)
    divisor = jax.random.randint(key_count, (PROW * PCOL,), 1, 5)
    counts = (K_MAX // divisor).astype(jnp.int32)
    chosen = jax.random.randint(key_pick, (), 0, PROW * PCOL)
    counts = jnp.where(jnp.arange(PROW * PCOL) == chosen, K_MAX, counts)
    return counts.reshape(PROW, PCOL).astype(jnp.int32)


def block_levels(key, shape, shards, smallest, high):
    factor_of = 1.0
    for dim, parts in shards:
        heights = jax.random.uniform(jax.random.fold_in(jax.random.fold_in(key, 6), dim), (parts,), jnp.float32, smallest / len(shards), high / len(shards))
        factor_of = factor_of * jnp.repeat(jnp.exp(heights), shape[dim] // parts).reshape((-1,) + (1,) * (len(shape) - 1 - dim))
    return factor_of


def gaussian(stream_key, dims, width, bound, cuts=(), held_as=jnp.bfloat16):
    result = jax.random.normal(stream_key, dims, jnp.float32) * width
    if len(cuts) > 0:
        result = block_levels(stream_key, dims, cuts, -0.22, 0.18) * result
    return jnp.clip(result, min=-bound, max=bound).astype(held_as)


def setup_inputs(seed: int = 0) -> dict:
    keys = jax.random.split(jax.random.key(seed), 9)
    grad_out = gaussian(keys[0], (PROW, ROW_TILES * TILE, F), 1.0, 6.0, ((0, 16), (1, 16)))
    preact = gaussian(keys[1], (PROW, ROW_TILES * TILE, F), 2.0, 8.0, ((0, 16), (1, 16)))
    features = gaussian(keys[2], (PCOL, COL_TILES * TILE, F), 1.0, 6.0, ((0, 16), (1, 16)))
    weight = gaussian(keys[3], (F, F), F ** -0.5, 0.1875)
    tile_values = gaussian(keys[4], (PROW, PCOL, K_MAX, TILE, TILE), (TILE * max(1, N_ROW * K_MAX // (2 * COL_TILES))) ** -0.5, 0.125, ((0, 16), (1, 16)))
    tile_row = draw_tile_row(jax.random.fold_in(keys[8], 71), 0)
    tile_col = draw_tile_col(jax.random.fold_in(keys[8], 71), 0)
    tile_count = draw_tile_count(jax.random.fold_in(keys[8], 71), 0)
    return dict(grad_out=grad_out, preact=preact, features=features, weight=weight, tile_values=tile_values, tile_row=tile_row, tile_col=tile_col, tile_count=tile_count)


def silu_grad(grad_out, preact):
    pre_value = preact.astype(jnp.float32)
    sigmoid_val = jax.nn.sigmoid(pre_value)
    scaled = grad_out.astype(jnp.float32) * sigmoid_val * (1.0 + pre_value * (1.0 - sigmoid_val))
    return scaled.astype(jnp.bfloat16)

def reference(grad_out, preact, features, weight, tile_values, tile_row, tile_col, tile_count):
    grad_pre = silu_grad(grad_out, preact).reshape(PROW, ROW_TILES, TILE, F)
    flat_values = tile_values.reshape(PROW * PCOL, K_MAX, TILE, TILE)
    flat_rows = tile_row.reshape(PROW * PCOL, K_MAX)
    flat_cols = tile_col.reshape(PROW * PCOL, K_MAX)
    flat_count = tile_count.reshape(PROW * PCOL)

    def device_term(running, device_idx):
        row_index = device_idx // PCOL
        col_index = device_idx % PCOL
        picked = grad_pre[row_index][flat_rows[device_idx]]
        product = jnp.einsum('kab,kaf->kbf', flat_values[device_idx].astype(jnp.float32), picked.astype(jnp.float32))
        live_mask = jnp.arange(K_MAX, dtype=jnp.int32) < flat_count[device_idx]
        product = jnp.where(live_mask[:, None, None], product, 0.0)
        partial_sum = jnp.zeros((COL_TILES, TILE, F), jnp.float32).at[flat_cols[device_idx]].add(product)
        rounded = lax.optimization_barrier(partial_sum.astype(jnp.bfloat16))
        return (running.at[col_index].add(rounded.astype(jnp.float32)), None)
    total, unused = lax.scan(device_term, jnp.zeros((PCOL, COL_TILES, TILE, F), jnp.float32), jnp.arange(PROW * PCOL, dtype=jnp.int32))
    mixed = total.reshape(PCOL * COL_TILES * TILE, F).astype(jnp.bfloat16)
    grad_in = lax.dot_general(mixed, weight, (((1,), (1,)), ((), ())), preferred_element_type=jnp.float32)
    grad_in = grad_in.astype(jnp.bfloat16).reshape(PCOL, COL_TILES * TILE, F)
    grad_weight = lax.dot_general(features.reshape(PCOL * COL_TILES * TILE, F), mixed, (((0,), (0,)), ((), ())), preferred_element_type=jnp.float32)
    return (grad_in, grad_weight)
```

```python
import jax
import jax.numpy as jnp
from jax import lax
from jax.experimental import pallas as pl
from jax.experimental.pallas import tpu as pltpu
from jax.sharding import Mesh, PartitionSpec as P

ROW = ("z", "yh")
COL = ("x", "yl", "core")
CHUNKS = 4
GROUP = 8
PARTS = ((0, 1, 2), (3,))


def silu_grad(grad_out, preact):
    pre_value = preact.astype(jnp.float32)
    sigmoid_val = jax.nn.sigmoid(pre_value)
    scaled = grad_out.astype(jnp.float32) * sigmoid_val * (1.0 + pre_value * (1.0 - sigmoid_val))
    return scaled.astype(jnp.bfloat16)


def tile_kernel(count_ref, row_ref, col_ref, blocks_ref, panel_ref, out_ref, total):
    tiles, size, width = total.shape
    tiles = tiles - 1
    slots = blocks_ref.shape[0]
    count = count_ref[0]
    total[...] = jnp.zeros_like(total)

    def add_group(step, carry):
        products = []
        for u in range(GROUP):
            slot = step * GROUP + u
            start = pl.multiple_of(row_ref[slot] * size, size)
            products.append(lax.dot_general(
                blocks_ref[slot], panel_ref[pl.ds(start, size), :], (((0,), (0,)), ((), ())),
                preferred_element_type=jnp.float32,
            ))
        for u in range(GROUP):
            slot = step * GROUP + u
            place = jnp.where(slot < count, col_ref[slot], tiles)
            total[place] += products[u]
        return carry

    lax.fori_loop(0, (count + GROUP - 1) // GROUP, add_group, 0)

    def store(tile, carry):
        out_ref[tile] = total[tile].astype(out_ref.dtype)
        return carry

    lax.fori_loop(0, tiles, store, 0)


def tile_sum(panel, blocks, row_ids, col_ids, used_count, col_tiles):
    slots, size, _ = blocks.shape
    width = panel.shape[1]
    pad = -slots % GROUP
    if pad:
        blocks = jnp.pad(blocks, ((0, pad), (0, 0), (0, 0)))
        row_ids, col_ids = jnp.pad(row_ids, (0, pad)), jnp.pad(col_ids, (0, pad))
    return pl.pallas_call(
        tile_kernel,
        out_shape=jax.ShapeDtypeStruct((col_tiles, size, width), jnp.bfloat16),
        in_specs=[pl.BlockSpec(memory_space=pltpu.SMEM)] * 3 + [pl.BlockSpec(memory_space=pltpu.VMEM)] * 2,
        out_specs=pl.BlockSpec(memory_space=pltpu.VMEM),
        scratch_shapes=[pltpu.VMEM((col_tiles + 1, size, width), jnp.float32)],
        compiler_params=pltpu.CompilerParams(vmem_limit_bytes=40 * 2**20),
        cost_estimate=pl.CostEstimate(
            flops=2 * slots * size * size * width,
            bytes_accessed=2 * (blocks.size + panel.size + col_tiles * size * width),
            transcendentals=0,
        ),
    )(used_count, row_ids, col_ids, blocks, panel)


def row_sum(partial, ways):
    size = lax.axis_size("z")
    here = lax.axis_index("z")
    pieces = partial.reshape(size, -1, partial.shape[-1])

    def own(place):
        return lax.dynamic_index_in_dim(pieces, jnp.bitwise_and(place, size - 1), 0, keepdims=False)

    arrived = []
    for way, hops in ways:
        perm = [(i, (i + way) % size) for i in range(size)]
        moving = own(here + way * hops)
        for hop in range(hops, 0, -1):
            moving = lax.ppermute(moving, "z", perm)
            if hop > 1:
                moving = (moving.astype(jnp.float32) + own(here + way * (hop - 1)).astype(jnp.float32)).astype(jnp.bfloat16)
        arrived.append(moving)
    arrived.append(own(here))
    half = lax.axis_index("yh")

    def total(which):
        halves = [lax.dynamic_index_in_dim(t.reshape(2, -1, t.shape[-1]), which, 0, keepdims=False) for t in arrived]
        return sum(t.astype(jnp.float32) for t in halves)

    other = lax.ppermute(total(1 - half).astype(jnp.bfloat16), "yh", [(0, 1), (1, 0)])
    return (total(half) + other.astype(jnp.float32)).astype(jnp.bfloat16)


def sum_everywhere(terms):
    rows = lax.axis_size(ROW)
    cols = lax.axis_size(COL)
    cores = lax.axis_size("core")
    n = len(terms)
    stack = jnp.stack([t.astype(jnp.bfloat16) for t in terms])
    height, width = terms[0].shape
    size = (height * cores) // (rows * cols)
    lanes = width // cores
    stack = stack.reshape(n, rows, cols // cores, size, cores, lanes)
    stack = stack.transpose(2, 4, 1, 0, 3, 5).reshape(cols, rows, n, size, lanes)
    first = lax.all_to_all(stack, COL, 0, 0, tiled=True)
    first = jnp.sum(first.astype(jnp.float32), axis=0).astype(jnp.bfloat16)
    second = lax.all_to_all(first, ROW, 0, 0, tiled=True)
    second = jnp.sum(second.astype(jnp.float32), axis=0).astype(jnp.bfloat16)
    whole = lax.all_gather(second.reshape(n * size, lanes), COL, axis=0, tiled=True)
    whole = lax.all_gather(whole, ROW, axis=0, tiled=True)
    whole = whole.reshape(rows, cols // cores, cores, n, size, lanes)
    whole = whole.transpose(3, 0, 1, 4, 2, 5).reshape(n, height, width)
    return [whole[i].astype(jnp.float32) for i in range(n)]


def per_device(grad_out, preact, features, weight, tile_values, tile_row, tile_col, tile_count):
    width = grad_out.shape[-1] // CHUNKS
    col_tiles = features.shape[1] * lax.axis_size(ROW) // tile_values.shape[-1]
    mixed = []
    terms = []
    for c in range(CHUNKS):
        part = slice(c * width, (c + 1) * width)
        grad_pre = silu_grad(grad_out[0, :, part], preact[0, :, part])
        panel = lax.all_gather(grad_pre, COL, axis=0, tiled=True)
        partial = tile_sum(panel, tile_values[0, 0], tile_row[0, 0], tile_col[0, 0], tile_count[0], col_tiles)
        ways = ((1, 4), (-1, 3)) if c % 2 == 0 else ((1, 3), (-1, 4))
        mixed.append(row_sum(partial.reshape(-1, width), ways))
        terms.append(lax.dot_general(
            features[0], mixed[-1], (((0,), (0,)), ((), ())), preferred_element_type=jnp.float32
        ))
    grad_weight = []
    for members in PARTS:
        grad_weight += sum_everywhere([terms[c] for c in members])
    grad_in = lax.dot_general(
        jnp.concatenate(mixed, axis=1), weight, (((1,), (1,)), ((), ())), preferred_element_type=jnp.float32
    )
    return (grad_in.astype(jnp.bfloat16)[None], jnp.concatenate(grad_weight, axis=1))


def solution(mesh):
    devices = mesh.devices.reshape(8, 2, 4, 2, 2)
    fine = Mesh(devices, ROW + COL)
    return jax.shard_map(
        per_device,
        mesh=fine,
        in_specs=(
            P(ROW, COL, None),
            P(ROW, COL, None),
            P(COL, ROW, None),
            P(),
            P(ROW, COL, None, None, None),
            P(ROW, COL, None),
            P(ROW, COL, None),
            P(ROW, COL),
        ),
        out_specs=(P(COL, ROW, None), P()),
        check_vma=False,
    )
```

```python
import functools

import jax
import jax.numpy as jnp
from jax import lax
from jax.experimental import pallas as pl
from jax.experimental.pallas import tpu as pltpu
from jax.sharding import Mesh, PartitionSpec as P

ROW = ("z", "yh")
COL = ("x", "yl", "core")
PLANE = ("yh", "x", "yl", "core")
CHUNKS = 4
GROUP = 8
PERMUTED = 2
PARTS = ((0, 1), (2, 3))


def silu_grad(grad_out, preact):
    pre_value = preact.astype(jnp.float32)
    sigmoid_val = jax.nn.sigmoid(pre_value)
    scaled = grad_out.astype(jnp.float32) * sigmoid_val * (1.0 + pre_value * (1.0 - sigmoid_val))
    return scaled.astype(jnp.bfloat16)


def tile_kernel(column, count_ref, row_ref, col_ref, blocks_hbm, *rest):
    panels_hbm, (out_ref, total, blocks_ref, panel_ref, sems) = rest[:-5], rest[-5:]
    tiles, size, width = total.shape
    tiles = tiles - 1
    count = count_ref[0]
    copies = [pltpu.make_async_copy(blocks_hbm, blocks_ref, sems.at[0])]
    depth = panel_ref.shape[0] // len(panels_hbm)
    for i, panel in enumerate(panels_hbm):
        copies.append(pltpu.make_async_copy(
            panel.at[:, pl.ds(column, width)], panel_ref.at[pl.ds(i * depth, depth)], sems.at[i + 1]
        ))
    for copy in copies:
        copy.start()
    total[...] = jnp.zeros_like(total)
    for copy in copies:
        copy.wait()

    def add_group(step, carry):
        products = []
        for u in range(GROUP):
            slot = step * GROUP + u
            start = pl.multiple_of(row_ref[slot] * size, size)
            products.append(lax.dot_general(
                blocks_ref[slot], panel_ref[pl.ds(start, size), :], (((0,), (0,)), ((), ())),
                preferred_element_type=jnp.float32,
            ))
        for u in range(GROUP):
            slot = step * GROUP + u
            place = jnp.where(slot < count, col_ref[slot], tiles)
            total[place] += products[u]
        return carry

    lax.fori_loop(0, (count + GROUP - 1) // GROUP, add_group, 0)

    def store(tile, carry):
        out_ref[tile] = total[tile].astype(out_ref.dtype)
        return carry

    lax.fori_loop(0, tiles, store, 0)


def tile_sum(panels, column, width, blocks, row_ids, col_ids, used_count, col_tiles):
    slots, size, _ = blocks.shape
    depth = sum(p.shape[0] for p in panels)
    return pl.pallas_call(
        functools.partial(tile_kernel, column),
        out_shape=jax.ShapeDtypeStruct((col_tiles, size, width), jnp.bfloat16),
        in_specs=[pl.BlockSpec(memory_space=pltpu.SMEM)] * 3 + [pl.BlockSpec(memory_space=pl.ANY)] * (1 + len(panels)),
        out_specs=pl.BlockSpec(memory_space=pltpu.VMEM),
        scratch_shapes=[
            pltpu.VMEM((col_tiles + 1, size, width), jnp.float32),
            pltpu.VMEM(blocks.shape, jnp.bfloat16),
            pltpu.VMEM((depth, width), jnp.bfloat16),
            pltpu.SemaphoreType.DMA((1 + len(panels),)),
        ],
        compiler_params=pltpu.CompilerParams(vmem_limit_bytes=32 * 2**20),
        cost_estimate=pl.CostEstimate(
            flops=2 * slots * size * size * width,
            bytes_accessed=2 * (blocks.size + depth * width + col_tiles * size * width),
            transcendentals=0,
        ),
    )(used_count, row_ids, col_ids, blocks, *panels)


def shift(value, axis, way):
    size = lax.axis_size(axis)
    return lax.ppermute(value, axis, [(i, (i + way) % size) for i in range(size)])


def gather_panel(mine):
    pair = jnp.concatenate([mine, shift(mine, "yl", 1)])
    left = shift(pair, "x", 1)
    right = shift(pair, "x", -1)
    rows = mine.shape[0]
    far = [shift(left[:rows], "x", 1), shift(right[rows:], "x", -1)]
    own = jnp.concatenate([pair, left, right] + far)
    return own, shift(own, "core", 1)


def gathered_place(tile_row, per_shard):
    shard, inner = tile_row // per_shard, tile_row % per_shard
    x, yl, core = shard // 4, (shard // 2) % 2, shard % 2
    away = (x - lax.axis_index("x")) % 4
    order = jnp.where(away == 3, 1, jnp.where(away == 0, 0, away + 1))
    other_yl = jnp.bitwise_xor(yl, lax.axis_index("yl"))
    other_core = jnp.bitwise_xor(core, lax.axis_index("core"))
    return ((other_core * 4 + order) * 2 + other_yl) * per_shard + inner


def row_sum(partial, ways):
    size = lax.axis_size("z")
    here = lax.axis_index("z")
    pieces = partial.reshape(size, -1, partial.shape[-1])

    def own(place):
        return lax.dynamic_index_in_dim(pieces, jnp.bitwise_and(place, size - 1), 0, keepdims=False)

    arrived = []
    for way, hops in ways:
        perm = [(i, (i + way) % size) for i in range(size)]
        moving = own(here + way * hops)
        for hop in range(hops, 0, -1):
            moving = lax.ppermute(moving, "z", perm)
            if hop > 1:
                moving = (moving.astype(jnp.float32) + own(here + way * (hop - 1)).astype(jnp.float32)).astype(jnp.bfloat16)
        arrived.append(moving)
    arrived.append(own(here))
    half = lax.axis_index("yh")

    def total(which):
        halves = [lax.dynamic_index_in_dim(t.reshape(2, -1, t.shape[-1]), which, 0, keepdims=False) for t in arrived]
        return sum(t.astype(jnp.float32) for t in halves)

    other = lax.ppermute(total(1 - half).astype(jnp.bfloat16), "yh", [(0, 1), (1, 0)])
    return (total(half) + other.astype(jnp.float32)).astype(jnp.bfloat16)


LANES = 128


def term_kernel(size, features_ref, *rest):
    mixed_refs, out_ref = rest[:-1], rest[-1]
    per_block = LANES // size
    for c, mixed_ref in enumerate(mixed_refs):
        halves = mixed_ref.shape[1] // LANES
        for block in range(features_ref.shape[1] // LANES):
            product = lax.dot_general(
                features_ref[:, block * LANES:(block + 1) * LANES], mixed_ref[...], (((0,), (0,)), ((), ())),
                preferred_element_type=jnp.float32,
            ).astype(out_ref.dtype)
            for r in range(per_block):
                for h in range(halves):
                    piece = product[r * size:(r + 1) * size, h * LANES:(h + 1) * LANES]
                    out_ref[(block * per_block + r) * halves + h, c] = piece


def weight_terms(features, mixed, plane):
    height, width = features.shape[1], mixed[0].shape[1]
    size = height * (width // LANES) // plane
    return pl.pallas_call(
        functools.partial(term_kernel, size),
        out_shape=jax.ShapeDtypeStruct((plane, len(mixed), size, LANES), jnp.bfloat16),
        in_specs=[pl.BlockSpec(memory_space=pltpu.VMEM)] * (1 + len(mixed)),
        out_specs=pl.BlockSpec(memory_space=pltpu.VMEM),
        cost_estimate=pl.CostEstimate(
            flops=2 * features.size * width * len(mixed),
            bytes_accessed=2 * (features.size + (features.shape[0] + height) * width * len(mixed)),
            transcendentals=0,
        ),
    )(features, *mixed)


def assemble_kernel(*refs):
    out_ref = refs[-1]
    column = 0
    for ref in refs[:-1]:
        places, chunks, size, lanes = ref.shape
        halves = places * size // out_ref.shape[0]
        for c in range(chunks):
            for h in range(halves):
                for r in range(places // halves):
                    out_ref[r * size:(r + 1) * size, column:column + lanes] = ref[r * halves + h, c].astype(out_ref.dtype)
                column += lanes


def assemble(parts, height):
    steps = 4
    width = sum(p.size for p in parts) // height
    return pl.pallas_call(
        assemble_kernel,
        grid=(steps,),
        out_shape=jax.ShapeDtypeStruct((height, width), jnp.float32),
        in_specs=[pl.BlockSpec((p.shape[0] // steps,) + p.shape[1:], lambda i: (i, 0, 0, 0)) for p in parts],
        out_specs=pl.BlockSpec((height // steps, width), lambda i: (i, 0)),
        cost_estimate=pl.CostEstimate(flops=0, bytes_accessed=6 * height * width, transcendentals=0),
    )(*parts)


def sum_everywhere(terms):
    plane = lax.axis_size(PLANE)
    depth = lax.axis_size("z")
    part = lax.all_to_all(terms, PLANE, 0, 0, tiled=True)
    part = jnp.sum(part.astype(jnp.float32), axis=0).astype(jnp.bfloat16)
    part = lax.all_to_all(jnp.broadcast_to(part[None], (depth,) + part.shape), "z", 0, 0, tiled=True)
    part = jnp.sum(part.astype(jnp.float32), axis=0).astype(jnp.bfloat16)
    return lax.all_to_all(jnp.broadcast_to(part[None], (plane,) + part.shape), PLANE, 0, 0, tiled=True)


def per_device(grad_out, preact, features, weight, tile_values, tile_row, tile_col, tile_count):
    width = grad_out.shape[-1] // CHUNKS
    size = tile_values.shape[-1]
    col_tiles = features.shape[1] * lax.axis_size(ROW) // size
    blocks, rows, cols, count = tile_values[0, 0], tile_row[0, 0], tile_col[0, 0], tile_count[0]

    def grad_pre(first, last):
        part = slice(first * width, last * width)
        return silu_grad(grad_out[0, :, part], preact[0, :, part])

    early = [grad_pre(c, c + 1) for c in range(PERMUTED)]
    early, late = lax.optimization_barrier((early, grad_pre(PERMUTED, CHUNKS)))
    places = gathered_place(rows, grad_out.shape[1] // size)
    sources = [(gather_panel(g), 0, places) for g in early]
    late = lax.all_gather(late, COL, axis=0, tiled=True)
    sources += [((late,), c * width, rows) for c in range(CHUNKS - PERMUTED)]
    mixed = []
    for c, (panels, column, where) in enumerate(sources):
        partial = tile_sum(panels, column, width, blocks, where, cols, count, col_tiles)
        ways = ((1, 4), (-1, 3)) if c % 2 == 0 else ((1, 3), (-1, 4))
        mixed.append(row_sum(partial.reshape(-1, width), ways))
    parts = [
        sum_everywhere(weight_terms(features[0], [mixed[c] for c in members], lax.axis_size(PLANE)))
        for members in PARTS
    ]
    grad_in = lax.dot_general(
        jnp.concatenate(mixed, axis=1), weight, (((1,), (1,)), ((), ())), preferred_element_type=jnp.float32
    )
    return (grad_in.astype(jnp.bfloat16)[None], assemble(parts, features.shape[-1]))


def solution(mesh):
    devices = mesh.devices.reshape(8, 2, 4, 2, 2)
    fine = Mesh(devices, ROW + COL)
    return jax.shard_map(
        per_device,
        mesh=fine,
        in_specs=(
            P(ROW, COL, None),
            P(ROW, COL, None),
            P(COL, ROW, None),
            P(),
            P(ROW, COL, None, None, None),
            P(ROW, COL, None),
            P(ROW, COL, None),
            P(ROW, COL),
        ),
        out_specs=(P(COL, ROW, None), P()),
        check_vma=False,
    )
```

```python
import functools

import jax
import jax.numpy as jnp
from jax import lax
from jax.experimental import pallas as pl
from jax.experimental.pallas import tpu as pltpu
from jax.sharding import Mesh, PartitionSpec as P

ROW = ("z", "yh")
COL = ("x", "yl", "core")
SIDE = ("yh", "x", "yl")
GROUP = 8
STEP = 256
CHUNKS = 2
REACH = 3


def silu_grad(grad_out, preact):
    pre_value = preact.astype(jnp.float32)
    sigmoid_val = jax.nn.sigmoid(pre_value)
    scaled = grad_out.astype(jnp.float32) * sigmoid_val * (1.0 + pre_value * (1.0 - sigmoid_val))
    return scaled.astype(jnp.bfloat16)


def tile_kernel(column, count_ref, row_ref, col_ref, blocks_hbm, panel_hbm, *rest):
    out_ref, total, blocks_ref, panel_ref, sems = rest[-5:]
    tiles, size, width = total.shape
    tiles = tiles - 1
    count = count_ref[0]
    copies = [
        pltpu.make_async_copy(blocks_hbm, blocks_ref, sems.at[0]),
        pltpu.make_async_copy(panel_hbm.at[:, pl.ds(column, width)], panel_ref, sems.at[1]),
    ]
    for copy in copies:
        copy.start()
    total[...] = jnp.zeros_like(total)
    for copy in copies:
        copy.wait()

    def add_group(step, carry):
        products = []
        for u in range(GROUP):
            slot = step * GROUP + u
            start = pl.multiple_of(row_ref[slot] * size, size)
            products.append(lax.dot_general(
                blocks_ref[slot], panel_ref[pl.ds(start, size), :], (((0,), (0,)), ((), ())),
                preferred_element_type=jnp.float32,
            ))
        for u in range(GROUP):
            slot = step * GROUP + u
            place = jnp.where(slot < count, col_ref[slot], tiles)
            total[place] += products[u]
        return carry

    lax.fori_loop(0, (count + GROUP - 1) // GROUP, add_group, 0)

    def store(tile, carry):
        out_ref[tile] = total[tile].astype(out_ref.dtype)
        return carry

    lax.fori_loop(0, tiles, store, 0)


def tile_sum(panel, column, width, blocks, row_ids, col_ids, used_count, col_tiles, after):
    slots, size, _ = blocks.shape
    depth = panel.shape[0]
    return pl.pallas_call(
        functools.partial(tile_kernel, column),
        out_shape=jax.ShapeDtypeStruct((col_tiles, size, width), jnp.bfloat16),
        in_specs=[pl.BlockSpec(memory_space=pltpu.SMEM)] * 3 + [pl.BlockSpec(memory_space=pltpu.HBM)] * 2
        + [pl.BlockSpec(memory_space=pl.ANY)] * len(after),
        out_specs=pl.BlockSpec(memory_space=pltpu.VMEM),
        scratch_shapes=[
            pltpu.VMEM((col_tiles + 1, size, width), jnp.float32),
            pltpu.VMEM(blocks.shape, jnp.bfloat16),
            pltpu.VMEM((depth, width), jnp.bfloat16),
            pltpu.SemaphoreType.DMA((2,)),
        ],
        compiler_params=pltpu.CompilerParams(vmem_limit_bytes=28 * 2**20),
        cost_estimate=pl.CostEstimate(
            flops=2 * slots * size * size * width,
            bytes_accessed=2 * (blocks.size + depth * width + col_tiles * size * width),
            transcendentals=0,
        ),
    )(used_count, row_ids, col_ids, blocks, panel, *after)


def shift(value, axis, way):
    size = lax.axis_size(axis)
    return lax.ppermute(value, axis, [(i, (i + way) % size) for i in range(size)])


def row_sum(partial, ways, reach):
    size = lax.axis_size("z")
    here = lax.axis_index("z")

    def own(place):
        return lax.dynamic_index_in_dim(partial, jnp.bitwise_and(place, size - 1), 0, keepdims=False)

    arrived = []
    passing = {}
    sent = {}
    for way, hops in ways:
        moving = own(here + way * hops)
        if hops == reach:
            passing[way * reach] = moving
        for hop in range(hops, 0, -1):
            sent.setdefault(hop, []).append(moving)
            moving = shift(moving, "z", way)
            if hop > 1:
                moving = (moving.astype(jnp.float32) + own(here + way * (hop - 1)).astype(jnp.float32)).astype(jnp.bfloat16)
            if hop == reach + 1:
                passing[way * reach] = moving
        arrived.append(moving)
    arrived.append(own(here))
    half = lax.axis_index("yh")

    def total(which):
        halves = [lax.dynamic_index_in_dim(t.reshape(2, -1, t.shape[-1]), which, 0, keepdims=False) for t in arrived]
        return sum(t.astype(jnp.float32) for t in halves)

    other = shift(total(1 - half).astype(jnp.bfloat16), "yh", 1)
    mixed = (total(half) + other.astype(jnp.float32)).astype(jnp.bfloat16)
    return mixed, passing, sent


def gather_features(turned, reach):
    found = []
    for start in (turned, shift(turned, "yh", 1)):
        near = {0: start}
        for k in range(1, reach + 1):
            near[k] = shift(near[k - 1], "z", -1)
            near[-k] = shift(near[1 - k], "z", 1)
        found.append(near)
    return found


def term_kernel(reach, place_ref, partial, below, above, *refs):
    distances = list(range(-reach, reach + 1))
    features = [dict(zip(distances, refs[:len(distances)])), dict(zip(distances, refs[len(distances):]))]
    out_ref, own, sems = refs[-3:]
    copies = []
    for i, k in enumerate(distances[1:-1]):
        place = jnp.bitwise_and(place_ref[0] + k, partial.shape[0] - 1)
        copies.append(pltpu.make_async_copy(partial.at[place], own.at[i], sems.at[i]))
    for copy in copies:
        copy.start()
    for copy in copies:
        copy.wait()
    depth = features[0][0].shape[1]

    def block(step, carry):
        rows = pl.ds(pl.multiple_of(step * STEP, STEP), STEP)
        total = jnp.zeros((STEP, out_ref.shape[1]), jnp.float32)
        for h in range(2):
            half = jnp.bitwise_xor(place_ref[1], h)
            at = pl.ds(pl.multiple_of(half * depth, depth), depth)
            for i, k in enumerate(distances):
                if k == -reach:
                    nodes = below[at, :]
                elif k == reach:
                    nodes = above[at, :]
                else:
                    nodes = own[i - 1, at, :]
                total += jnp.dot(features[h][k][rows, :], nodes, preferred_element_type=jnp.float32)
        out_ref[rows, :] = total.astype(out_ref.dtype)
        return carry

    lax.fori_loop(0, out_ref.shape[0] // STEP, block, 0)


def weight_terms(features, reach, partial, passing):
    distances = list(range(-reach, reach + 1))
    height = features[0][0].shape[0]
    rows, width = partial.shape[1:]
    vmem = pl.BlockSpec(memory_space=pltpu.VMEM)
    return pl.pallas_call(
        functools.partial(term_kernel, reach),
        out_shape=jax.ShapeDtypeStruct((height, width), jnp.bfloat16),
        in_specs=[pl.BlockSpec(memory_space=pltpu.SMEM), pl.BlockSpec(memory_space=pl.ANY)]
        + [vmem] * (2 + 2 * len(distances)),
        out_specs=vmem,
        scratch_shapes=[
            pltpu.VMEM((2 * reach - 1, rows, width), jnp.bfloat16),
            pltpu.SemaphoreType.DMA((2 * reach - 1,)),
        ],
        compiler_params=pltpu.CompilerParams(vmem_limit_bytes=28 * 2**20),
        cost_estimate=pl.CostEstimate(
            flops=2 * height * rows * width * len(distances),
            bytes_accessed=2 * (height * rows * len(distances) + (rows * len(distances) + height) * width),
            transcendentals=0,
        ),
    )(
        jnp.stack([lax.axis_index("z"), lax.axis_index("yh")]), partial, passing[-reach], passing[reach],
        *[near[k] for near in features for k in distances],
    )


def sum_everywhere(terms, sent):
    side = lax.axis_size(SIDE)
    depth = lax.axis_size("z")
    core = lax.axis_index("core")
    halves = []
    for term in terms:
        term = term.reshape(2, -1, term.shape[-1])
        mine = lax.dynamic_index_in_dim(term, core, 0, keepdims=False)
        other = shift(lax.dynamic_index_in_dim(term, 1 - core, 0, keepdims=False), "core", 1)
        halves.append((mine.astype(jnp.float32) + other.astype(jnp.float32)).astype(jnp.bfloat16))
    part = jnp.concatenate(halves, axis=1)
    part = lax.all_to_all(part.reshape(side, -1, part.shape[-1]), SIDE, 0, 0, tiled=True)
    part = jnp.sum(part.astype(jnp.float32), axis=0).astype(jnp.bfloat16)
    part, _ = lax.optimization_barrier((part, sent[2]))
    part = lax.all_to_all(jnp.broadcast_to(part[None], (depth,) + part.shape), "z", 0, 0, tiled=True)
    part = jnp.sum(part.astype(jnp.float32), axis=0).astype(jnp.bfloat16)
    part, _ = lax.optimization_barrier((part, sent[1]))
    half = lax.all_to_all(jnp.broadcast_to(part[None], (side,) + part.shape), SIDE, 0, 0, tiled=True)
    half = half.reshape(-1, half.shape[-1])
    other = shift(half, "core", 1)
    low = jnp.where(core == 0, half, other)
    high = jnp.where(core == 0, other, half)
    return jnp.concatenate([low, high]).astype(jnp.float32)


def per_device(grad_out, preact, features, weight, tile_values, tile_row, tile_col, tile_count):
    size = tile_values.shape[-1]
    width = grad_out.shape[-1] // CHUNKS
    col_tiles = features.shape[1] * lax.axis_size(ROW) // size
    tiles = (tile_values[0, 0], tile_row[0, 0], tile_col[0, 0], tile_count[0], col_tiles)

    panel = lax.all_gather(silu_grad(grad_out[0], preact[0]), COL, axis=0, tiled=True)
    own, other = gather_features(features[0].T, REACH)
    order = (
        [own[2], own[-2], other[1], other[-1]],
        [own[3], own[-3], other[2], other[-2]],
    )
    partials = []
    mixed = []
    terms = []
    sent = {}
    for c in range(CHUNKS):
        partial = tile_sum(panel, c * width, width, *tiles, order[c] + partials)
        partials.append(partial)
        partial = partial.reshape(lax.axis_size("z"), -1, width)
        ways = ((1, 4), (-1, 3)) if c % 2 == 0 else ((1, 3), (-1, 4))
        total, passing, moves = row_sum(partial, ways, REACH)
        for hop, sums in moves.items():
            sent.setdefault(hop, []).extend(sums)
        mixed.append(total)
        terms.append(weight_terms((own, other), REACH, partial, passing))
    grad_weight = sum_everywhere(terms, sent)
    grad_in = lax.dot_general(
        jnp.concatenate(mixed, axis=1), weight, (((1,), (1,)), ((), ())), preferred_element_type=jnp.float32
    )
    return (grad_in.astype(jnp.bfloat16)[None], grad_weight)


def solution(mesh):
    devices = mesh.devices.reshape(8, 2, 4, 2, 2)
    fine = Mesh(devices, ROW + COL)
    return jax.shard_map(
        per_device,
        mesh=fine,
        in_specs=(
            P(ROW, COL, None),
            P(ROW, COL, None),
            P(COL, ROW, None),
            P(),
            P(ROW, COL, None, None, None),
            P(ROW, COL, None),
            P(ROW, COL, None),
            P(ROW, COL),
        ),
        out_specs=(P(COL, ROW, None), P()),
        check_vma=False,
    )
```

```python
import functools

import jax
import jax.numpy as jnp
from jax import lax
from jax.experimental import pallas as pl
from jax.experimental.pallas import tpu as pltpu
from jax.sharding import Mesh, PartitionSpec as P

ROW = ("z", "yh")
COL = ("x", "yl", "core")
SIDE = ("yh", "x", "yl")
GROUP = 8
STEP = 256
CHUNKS = 2
REACH = 3


def silu_grad(grad_out, preact):
    pre_value = preact.astype(jnp.float32)
    sigmoid_val = jax.nn.sigmoid(pre_value)
    scaled = grad_out.astype(jnp.float32) * sigmoid_val * (1.0 + pre_value * (1.0 - sigmoid_val))
    return scaled.astype(jnp.bfloat16)


def tile_kernel(chunks, count_ref, send_ref, row_ref, col_ref, blocks_hbm, panel_hbm, *refs):
    outs, (total, blocks_ref, panel_ref, stage, sems) = refs[:-5], refs[-5:]
    _, tiles, size, width = stage.shape
    count = count_ref[0]
    loads = [pltpu.make_async_copy(blocks_hbm, blocks_ref, sems.at[0])]
    for c in range(chunks):
        loads.append(pltpu.make_async_copy(
            panel_hbm.at[:, c * width:(c + 1) * width], panel_ref.at[c], sems.at[1 + c]
        ))
    for copy in loads:
        copy.start()
    total[...] = jnp.zeros_like(total)
    loads[0].wait()
    leaving = []
    for c in range(chunks):
        loads[1 + c].wait()

        def add_group(step, carry):
            products = []
            for u in range(GROUP):
                slot = step * GROUP + u
                start = pl.multiple_of(row_ref[slot] * size, size)
                products.append(lax.dot_general(
                    blocks_ref[slot], panel_ref[c, pl.ds(start, size), :], (((0,), (0,)), ((), ())),
                    preferred_element_type=jnp.float32,
                ))
            for u in range(GROUP):
                slot = step * GROUP + u
                place = jnp.where(slot < count, col_ref[slot], tiles)
                total[place] += products[u]
            return carry

        lax.fori_loop(0, (count + GROUP - 1) // GROUP, add_group, 0)

        def store(tile, carry):
            stage[c, tile] = total[tile].astype(stage.dtype)
            total[tile] = jnp.zeros((size, width), jnp.float32)
            return carry

        lax.fori_loop(0, tiles, store, 0)
        whole, *pieces = outs[3 * c:3 * c + 3]
        first = 1 + chunks + 3 * c
        for i, ref in enumerate(pieces):
            start = send_ref[2 * c + i] * ref.shape[0]
            leaving.append(pltpu.make_async_copy(stage.at[c, pl.ds(start, ref.shape[0])], ref, sems.at[first + i]))
        leaving.append(pltpu.make_async_copy(stage.at[c], whole, sems.at[first + 2]))
        for copy in leaving[-3:]:
            copy.start()
    for copy in leaving:
        copy.wait()


def tile_sum(panel, chunks, blocks, row_ids, col_ids, used_count, col_tiles, send):
    slots, size, _ = blocks.shape
    depth = panel.shape[0]
    width = panel.shape[1] // chunks
    piece = col_tiles // lax.axis_size("z")
    hbm = pl.BlockSpec(memory_space=pl.ANY)
    outs = pl.pallas_call(
        functools.partial(tile_kernel, chunks),
        out_shape=[jax.ShapeDtypeStruct((n, size, width), jnp.bfloat16) for n in (col_tiles, piece, piece)] * chunks,
        in_specs=[pl.BlockSpec(memory_space=pltpu.SMEM)] * 4 + [hbm] * 2,
        out_specs=[hbm] * (3 * chunks),
        scratch_shapes=[
            pltpu.VMEM((col_tiles + 1, size, width), jnp.float32),
            pltpu.VMEM(blocks.shape, jnp.bfloat16),
            pltpu.VMEM((chunks, depth, width), jnp.bfloat16),
            pltpu.VMEM((chunks, col_tiles, size, width), jnp.bfloat16),
            pltpu.SemaphoreType.DMA((1 + 4 * chunks,)),
        ],
        compiler_params=pltpu.CompilerParams(vmem_limit_bytes=56 * 2**20),
        cost_estimate=pl.CostEstimate(flops=1, bytes_accessed=1, transcendentals=0),
    )(used_count, send, row_ids, col_ids, blocks, panel)
    return [outs[3 * c:3 * c + 3] for c in range(chunks)]


def behind(value, others):
    return lax.optimization_barrier((value, others))[0]


def shift(value, axis, way):
    size = lax.axis_size(axis)
    return lax.ppermute(value, axis, [(i, (i + way) % size) for i in range(size)])


def row_sum(partial, pieces, ways):
    size = lax.axis_size("z")
    here = lax.axis_index("z")

    def own(place):
        return lax.dynamic_index_in_dim(partial, jnp.bitwise_and(place, size - 1), 0, keepdims=False)

    arrived = []
    sent = [[] for _ in range(size // 2)]
    for moving, (way, hops) in zip(pieces, ways):
        for hop in range(hops):
            sent[hop].append(moving)
            moving = shift(moving, "z", way)
            left = hops - 1 - hop
            if left:
                moving = (moving.astype(jnp.float32) + own(here + way * left).astype(jnp.float32)).astype(jnp.bfloat16)
        arrived.append(moving)
    arrived.append(own(here))
    half = lax.axis_index("yh")

    def total(which):
        halves = [lax.dynamic_index_in_dim(t.reshape(2, -1, t.shape[-1]), which, 0, keepdims=False) for t in arrived]
        return sum(t.astype(jnp.float32) for t in halves)

    other = shift(total(1 - half).astype(jnp.bfloat16), "yh", 1)
    mixed = (total(half) + other.astype(jnp.float32)).astype(jnp.bfloat16)
    return mixed, sent


def gather_features(turned, reach):
    found = []
    for start in (turned, shift(turned, "yh", 1)):
        if found:
            start = behind(start, [found[0][1], found[0][-1]])
        near = {0: start}
        for k in range(1, reach + 1):
            near[k] = shift(near[k - 1], "z", -1)
            near[-k] = shift(near[1 - k], "z", 1)
        found.append(near)
    return found


def term_kernel(chunks, reach, place_ref, *refs):
    partials, refs = refs[:chunks], refs[chunks:]
    passing, refs = refs[:2 * chunks], refs[2 * chunks:]
    features, (out_ref, total, left, nodes, sems) = refs[:-5], refs[-5:]
    z, yh, first = place_ref[0], place_ref[1], place_ref[2]
    rows = out_ref.shape[0]
    count = 2 * reach + 1
    depth = features[0].shape[1]
    width = nodes.shape[2]
    groups = []
    used = 0
    for i in range(count):
        group = []
        for h in range(2):
            b = 2 * i + h
            at = slice(b * depth, (b + 1) * depth)
            source = features[h * count + i].at[pl.ds(pl.multiple_of(first * rows, rows), rows), :]
            group.append(pltpu.make_async_copy(source, left.at[:, at], sems.at[used]))
            used += 1
            half = pl.ds(pl.multiple_of(jnp.bitwise_xor(yh, h) * depth, depth), depth)
            for c in range(chunks):
                if abs(i - reach) == reach:
                    source = passing[2 * c + (i > reach)].at[half, :]
                else:
                    source = partials[c].at[jnp.bitwise_and(z + (i - reach), partials[c].shape[0] - 1), half, :]
                group.append(pltpu.make_async_copy(source, nodes.at[c, at, :], sems.at[used]))
                used += 1
        groups.append(group)
    for group in groups:
        for copy in group:
            copy.start()
    steps = [(0, 1), (1, 3), (3, 5), (5, count)]
    for step, (low, high) in enumerate(steps):
        for group in groups[low:high]:
            for copy in group:
                copy.wait()
        inner = slice(low * 2 * depth, high * 2 * depth)

        def block(index, carry):
            at = pl.ds(pl.multiple_of(index * STEP, STEP), STEP)
            for c in range(chunks):
                columns = slice(c * width, (c + 1) * width)
                product = jnp.dot(left[at, inner], nodes[c, inner, :], preferred_element_type=jnp.float32)
                if step:
                    product = total[at, columns] + product
                if step < len(steps) - 1:
                    total[at, columns] = product
                else:
                    out_ref[at, columns] = product.astype(out_ref.dtype)
            return carry

        lax.fori_loop(0, rows // STEP, block, 0)


def weight_terms(features, partials, passing, reach, place):
    distances = list(range(-reach, reach + 1))
    features = [near[k] for near in features for k in distances]
    height, depth = features[0].shape
    width = partials[0].shape[2]
    chunks = len(partials)
    blocks = len(features)
    operands = list(partials) + [p for pair in passing for p in pair] + features
    return pl.pallas_call(
        functools.partial(term_kernel, chunks, reach),
        out_shape=jax.ShapeDtypeStruct((height // 2, chunks * width), jnp.bfloat16),
        in_specs=[pl.BlockSpec(memory_space=pltpu.SMEM)] + [pl.BlockSpec(memory_space=pl.ANY)] * len(operands),
        out_specs=pl.BlockSpec(memory_space=pltpu.VMEM),
        scratch_shapes=[
            pltpu.VMEM((height // 2, chunks * width), jnp.float32),
            pltpu.VMEM((height // 2, blocks * depth), jnp.bfloat16),
            pltpu.VMEM((chunks, blocks * depth, width), jnp.bfloat16),
            pltpu.SemaphoreType.DMA(((1 + chunks) * blocks,)),
        ],
        compiler_params=pltpu.CompilerParams(vmem_limit_bytes=56 * 2**20),
        cost_estimate=pl.CostEstimate(flops=1, bytes_accessed=1, transcendentals=0),
    )(place, *operands)


def assemble_kernel(core_ref, mine_ref, other_ref, out_ref):
    mine = core_ref[0] == pl.program_id(0)
    out_ref[...] = jnp.where(mine, mine_ref[...], other_ref[...]).astype(out_ref.dtype)


def assemble(mine, other):
    rows, width = mine.shape
    steps = 2
    half = pl.BlockSpec((rows // steps, width), lambda h, i: (i, 0))
    return pl.pallas_call(
        assemble_kernel,
        grid=(2, steps),
        out_shape=jax.ShapeDtypeStruct((2 * rows, width), jnp.float32),
        in_specs=[pl.BlockSpec(memory_space=pltpu.SMEM), half, half],
        out_specs=pl.BlockSpec((rows // steps, width), lambda h, i: (h * steps + i, 0)),
    )(lax.axis_index("core").reshape(1), mine, other)


def sum_everywhere(mine, other, second, third):
    side = lax.axis_size(SIDE)
    depth = lax.axis_size("z")
    part = mine.astype(jnp.float32) + shift(other, "core", 1).astype(jnp.float32)
    part = part.astype(jnp.bfloat16).reshape(side, -1, part.shape[-1])
    part = lax.all_to_all(part, SIDE, 0, 0, tiled=True)
    part = jnp.sum(part.astype(jnp.float32), axis=0).astype(jnp.bfloat16)
    part = behind(part, second)
    part = lax.all_to_all(jnp.broadcast_to(part[None], (depth,) + part.shape), "z", 0, 0, tiled=True)
    part = jnp.sum(part.astype(jnp.float32), axis=0).astype(jnp.bfloat16)
    part = behind(part, third)
    half = lax.all_to_all(jnp.broadcast_to(part[None], (side,) + part.shape), SIDE, 0, 0, tiled=True)
    half = half.reshape(-1, half.shape[-1])
    return assemble(half, shift(half, "core", 1))


def per_device(grad_out, preact, features, weight, tile_values, tile_row, tile_col, tile_count):
    size = tile_values.shape[-1]
    width = grad_out.shape[-1] // CHUNKS
    col_tiles = features.shape[1] * lax.axis_size(ROW) // size
    tiles = (tile_values[0, 0], tile_row[0, 0], tile_col[0, 0], tile_count[0], col_tiles)
    z, depth = lax.axis_index("z"), lax.axis_size("z")

    panel = lax.all_gather(silu_grad(grad_out[0], preact[0]), COL, axis=0, tiled=True)
    near = gather_features(features[0].T, REACH)
    ways = (((1, 4), (-1, 3)), ((1, 3), (-1, 4)))
    send = jnp.stack([jnp.bitwise_and(z + way * hops, depth - 1) for pair in ways for way, hops in pair])
    send = behind(send, [near[1][2], near[1][-2]])
    partials = []
    passing = []
    mixed = []
    sent = [[] for _ in range(depth // 2)]
    for (whole, *pieces), pair in zip(tile_sum(panel, CHUNKS, *tiles, send), ways):
        partials.append(whole.reshape(depth, -1, width))
        total, moves = row_sum(partials[-1], [p.reshape(-1, width) for p in pieces], pair)
        mixed.append(total)
        for hop, sums in enumerate(moves):
            sent[hop] += sums
        far = {way: moves[hops - REACH][i] for i, (way, hops) in enumerate(pair)}
        passing.append((far[-1], far[1]))
    core = lax.axis_index("core")
    theirs, ours = [jnp.stack([z, lax.axis_index("yh"), half]) for half in (1 - core, core)]
    theirs = weight_terms(near, partials, passing, REACH, theirs)
    ours = weight_terms(near, partials, passing, REACH, behind(ours, [theirs] + sent[1]))
    grad_weight = sum_everywhere(ours, theirs, sent[2], sent[3])
    grad_in = lax.dot_general(
        jnp.concatenate(mixed, axis=1), weight, (((1,), (1,)), ((), ())), preferred_element_type=jnp.float32
    )
    return (grad_in.astype(jnp.bfloat16)[None], grad_weight)


def solution(mesh):
    devices = mesh.devices.reshape(8, 2, 4, 2, 2)
    fine = Mesh(devices, ROW + COL)
    return jax.shard_map(
        per_device,
        mesh=fine,
        in_specs=(
            P(ROW, COL, None),
            P(ROW, COL, None),
            P(COL, ROW, None),
            P(),
            P(ROW, COL, None, None, None),
            P(ROW, COL, None),
            P(ROW, COL, None),
            P(ROW, COL),
        ),
        out_specs=(P(COL, ROW, None), P()),
        check_vma=False,
    )
```

```python
import functools

import jax
import jax.numpy as jnp
from jax import lax
from jax.experimental import pallas as pl
from jax.experimental.pallas import tpu as pltpu
from jax.sharding import Mesh, PartitionSpec as P

ROW = ("z", "yh")
COL = ("x", "yl", "core")
SIDE = ("yh", "x", "yl")
GROUP = 8
CHUNKS = 2
REACH = 3


def silu_grad(grad_out, preact):
    pre_value = preact.astype(jnp.float32)
    sigmoid_val = jax.nn.sigmoid(pre_value)
    scaled = grad_out.astype(jnp.float32) * sigmoid_val * (1.0 + pre_value * (1.0 - sigmoid_val))
    return scaled.astype(jnp.bfloat16)


def tile_kernel(columns, count_ref, send_ref, row_ref, col_ref, blocks_hbm, panel_hbm, *refs):
    outs, (total, blocks_ref, panel_ref, stage, sems) = refs[:-5], refs[-5:]
    chunks = len(columns)
    _, tiles, size, width = stage.shape
    count = count_ref[0]
    loads = [pltpu.make_async_copy(blocks_hbm, blocks_ref, sems.at[0])]
    for c in range(chunks):
        loads.append(pltpu.make_async_copy(
            panel_hbm.at[:, columns[c]:columns[c] + width], panel_ref.at[c], sems.at[1 + c]
        ))
    for copy in loads:
        copy.start()
    total[...] = jnp.zeros_like(total)
    loads[0].wait()
    leaving = []
    for c in range(chunks):
        loads[1 + c].wait()

        def add_group(step, carry):
            for u in range(GROUP):
                slot = step * GROUP + u
                start = pl.multiple_of(row_ref[slot] * size, size)
                place = jnp.where(slot < count, col_ref[slot], tiles)
                total[place] += lax.dot_general(
                    blocks_ref[slot], panel_ref[c, pl.ds(start, size), :], (((0,), (0,)), ((), ())),
                    preferred_element_type=jnp.float32,
                )
            return carry

        lax.fori_loop(0, (count + GROUP - 1) // GROUP, add_group, 0)

        def store(tile, carry):
            stage[c, tile] = total[tile].astype(stage.dtype)
            if c < chunks - 1:
                total[tile] = jnp.zeros((size, width), jnp.float32)
            return carry

        lax.fori_loop(0, tiles, store, 0)
        whole, *pieces = outs[3 * c:3 * c + 3]
        first = 1 + chunks + 3 * c
        for i, ref in enumerate(pieces):
            start = send_ref[2 * c + i] * ref.shape[0]
            leaving.append(pltpu.make_async_copy(stage.at[c, pl.ds(start, ref.shape[0])], ref, sems.at[first + i]))
        leaving.append(pltpu.make_async_copy(stage.at[c], whole, sems.at[first + 2]))
        for copy in leaving[-3:]:
            copy.start()
    for copy in leaving:
        copy.wait()


def tile_sum(panel, columns, width, blocks, row_ids, col_ids, used_count, col_tiles, send):
    slots, size, _ = blocks.shape
    depth = panel.shape[0]
    chunks = len(columns)
    piece = col_tiles // lax.axis_size("z")
    hbm = pl.BlockSpec(memory_space=pl.ANY)
    outs = pl.pallas_call(
        functools.partial(tile_kernel, columns),
        out_shape=[jax.ShapeDtypeStruct((n, size, width), jnp.bfloat16) for n in (col_tiles, piece, piece)] * chunks,
        in_specs=[pl.BlockSpec(memory_space=pltpu.SMEM)] * 4 + [hbm] * 2,
        out_specs=[hbm] * (3 * chunks),
        scratch_shapes=[
            pltpu.VMEM((col_tiles + 1, size, width), jnp.float32),
            pltpu.VMEM(blocks.shape, jnp.bfloat16),
            pltpu.VMEM((chunks, depth, width), jnp.bfloat16),
            pltpu.VMEM((chunks, col_tiles, size, width), jnp.bfloat16),
            pltpu.SemaphoreType.DMA((1 + 4 * chunks,)),
        ],
        compiler_params=pltpu.CompilerParams(vmem_limit_bytes=56 * 2**20),
        cost_estimate=pl.CostEstimate(
            flops=2 * slots * size * size * width * chunks,
            bytes_accessed=2 * (blocks.size + depth * width * chunks + col_tiles * size * width * chunks),
            transcendentals=0,
        ),
    )(used_count, send, row_ids, col_ids, blocks, panel)
    return [outs[3 * c:3 * c + 3] for c in range(chunks)]


def behind(value, others):
    return lax.optimization_barrier((value, others))[0]


def shift(value, axis, way):
    size = lax.axis_size(axis)
    return lax.ppermute(value, axis, [(i, (i + way) % size) for i in range(size)])


def row_sum(partial, pieces, ways):
    size = lax.axis_size("z")
    here = lax.axis_index("z")

    def own(place):
        return lax.dynamic_index_in_dim(partial, jnp.bitwise_and(place, size - 1), 0, keepdims=False)

    arrived = []
    sent = [[] for _ in range(size // 2)]
    for moving, (way, hops) in zip(pieces, ways):
        for hop in range(hops):
            sent[hop].append(moving)
            moving = shift(moving, "z", way)
            left = hops - 1 - hop
            if left:
                moving = (moving.astype(jnp.float32) + own(here + way * left).astype(jnp.float32)).astype(jnp.bfloat16)
        arrived.append(moving)
    arrived.append(own(here))
    half = lax.axis_index("yh")

    def total(which):
        halves = [lax.dynamic_index_in_dim(t.reshape(2, -1, t.shape[-1]), which, 0, keepdims=False) for t in arrived]
        return sum(t.astype(jnp.float32) for t in halves)

    other = shift(total(1 - half).astype(jnp.bfloat16), "yh", 1)
    mixed = (total(half) + other.astype(jnp.float32)).astype(jnp.bfloat16)
    return mixed, sent


def gather_features(turned, reach):
    own = {0: turned}
    other = {0: shift(turned, "yh", 1)}
    for k in range(1, reach + 1):
        for near in (own, other):
            if near is other and k == reach:
                near[k], near[-k] = shift(own[k], "yh", 1), shift(own[-k], "yh", 1)
            else:
                near[k], near[-k] = shift(near[k - 1], "z", -1), shift(near[1 - k], "z", 1)
    return own, other


def term_kernel(chunks, reach, place_ref, *refs):
    partials, refs = refs[:chunks], refs[chunks:]
    passing, refs = refs[:2 * chunks], refs[2 * chunks:]
    features, (out_ref, total, left, nodes, sems) = refs[:-5], refs[-5:]
    z, yh, first = place_ref[0], place_ref[1], place_ref[2]
    rows = out_ref.shape[0]
    count = 2 * reach + 1
    depth = features[0].shape[1]
    width = nodes.shape[2]
    groups = []
    used = 0
    for i in range(count):
        group = []
        for h in range(2):
            b = 2 * i + h
            at = slice(b * depth, (b + 1) * depth)
            source = features[h * count + i].at[pl.ds(pl.multiple_of(first * rows, rows), rows), :]
            group.append(pltpu.make_async_copy(source, left.at[:, at], sems.at[used]))
            used += 1
            half = pl.ds(pl.multiple_of(jnp.bitwise_xor(yh, h) * depth, depth), depth)
            for c in range(chunks):
                if abs(i - reach) == reach:
                    source = passing[2 * c + (i > reach)].at[half, :]
                else:
                    source = partials[c].at[jnp.bitwise_and(z + (i - reach), partials[c].shape[0] - 1), half, :]
                group.append(pltpu.make_async_copy(source, nodes.at[c, at, :], sems.at[used]))
                used += 1
        groups.append(group)
    for group in groups:
        for copy in group:
            copy.start()
    steps = [(0, 1), (1, 3), (3, 5), (5, count)]
    for step, (low, high) in enumerate(steps):
        for group in groups[low:high]:
            for copy in group:
                copy.wait()
        inner = slice(low * 2 * depth, high * 2 * depth)

        for c in range(chunks):
            columns = slice(c * width, (c + 1) * width)
            product = jnp.dot(left[:, inner], nodes[c, inner, :], preferred_element_type=jnp.float32)
            if step:
                product = total[:, columns] + product
            if step < len(steps) - 1:
                total[:, columns] = product
            else:
                out_ref[:, columns] = product.astype(out_ref.dtype)


def weight_terms(features, partials, passing, reach, place):
    distances = list(range(-reach, reach + 1))
    features = [near[k] for near in features for k in distances]
    height, depth = features[0].shape
    width = partials[0].shape[2]
    chunks = len(partials)
    blocks = len(features)
    operands = list(partials) + [p for pair in passing for p in pair] + features
    return pl.pallas_call(
        functools.partial(term_kernel, chunks, reach),
        out_shape=jax.ShapeDtypeStruct((height // 2, chunks * width), jnp.bfloat16),
        in_specs=[pl.BlockSpec(memory_space=pltpu.SMEM)] + [pl.BlockSpec(memory_space=pl.ANY)] * len(operands),
        out_specs=pl.BlockSpec(memory_space=pltpu.VMEM),
        scratch_shapes=[
            pltpu.VMEM((height // 2, chunks * width), jnp.float32),
            pltpu.VMEM((height // 2, blocks * depth), jnp.bfloat16),
            pltpu.VMEM((chunks, blocks * depth, width), jnp.bfloat16),
            pltpu.SemaphoreType.DMA(((1 + chunks) * blocks,)),
        ],
        compiler_params=pltpu.CompilerParams(vmem_limit_bytes=56 * 2**20),
        cost_estimate=pl.CostEstimate(
            flops=height * blocks * depth * chunks * width,
            bytes_accessed=2 * blocks * depth * (height // 2 + chunks * width) + height * chunks * width,
            transcendentals=0,
        ),
    )(place, *operands)


def sum_everywhere(mine, other, second, third):
    side = lax.axis_size(SIDE)
    depth = lax.axis_size("z")
    part = mine.astype(jnp.float32) + shift(other, "core", 1).astype(jnp.float32)
    part = part.astype(jnp.bfloat16).reshape(side, -1, part.shape[-1])
    part = lax.all_to_all(part, SIDE, 0, 0, tiled=True)
    part = jnp.sum(part.astype(jnp.float32), axis=0).astype(jnp.bfloat16)
    part = behind(part, second)
    parts = [part] + [shift(part, "z", k) for k in range(1, depth)]
    part = sum(p.astype(jnp.float32) for p in parts).astype(jnp.bfloat16)
    part = behind(part, third)
    half = lax.all_to_all(jnp.broadcast_to(part[None], (side,) + part.shape), SIDE, 0, 0, tiled=True)
    half = half.reshape(-1, half.shape[-1])
    other = shift(half, "core", 1)
    first = lax.axis_index("core") == 0
    return jnp.concatenate([jnp.where(first, half, other), jnp.where(first, other, half)]).astype(jnp.float32)


def per_device(grad_out, preact, features, weight, tile_values, tile_row, tile_col, tile_count):
    size = tile_values.shape[-1]
    width = grad_out.shape[-1] // CHUNKS
    col_tiles = features.shape[1] * lax.axis_size(ROW) // size
    tiles = (tile_values[0, 0], tile_row[0, 0], tile_col[0, 0], tile_count[0], col_tiles)
    z, depth = lax.axis_index("z"), lax.axis_size("z")

    panel = lax.all_gather(silu_grad(grad_out[0], preact[0]), COL, axis=0, tiled=True)
    near = gather_features(features[0].T, REACH)
    ways = (((1, 4), (-1, 3)), ((1, 3), (-1, 4)))
    own, other = near
    before = [own[3], own[-3], other[1], other[-1]]
    partials = []
    passing = []
    mixed = []
    sent = [[] for _ in range(depth // 2)]
    for c, pair in enumerate(ways):
        send = jnp.stack([jnp.bitwise_and(z + way * hops, depth - 1) for way, hops in pair])
        ((whole, *pieces),) = tile_sum(panel, (c * width,), width, *tiles, behind(send, before))
        before = pieces + [other[k] for k in (2, -2, 3, -3)]
        partials.append(whole.reshape(depth, -1, width))
        total, moves = row_sum(partials[-1], [p.reshape(-1, width) for p in pieces], pair)
        mixed.append(total)
        for hop, sums in enumerate(moves):
            sent[hop] += sums
        far = {way: moves[hops - REACH][i] for i, (way, hops) in enumerate(pair)}
        passing.append((far[-1], far[1]))
    core = lax.axis_index("core")
    theirs, ours = [jnp.stack([z, lax.axis_index("yh"), half]) for half in (1 - core, core)]
    theirs = weight_terms(near, partials, passing, REACH, theirs)
    ours = weight_terms(near, partials, passing, REACH, behind(ours, theirs))
    grad_weight = sum_everywhere(ours, theirs, sent[2], sent[3])
    grad_in = lax.dot_general(
        jnp.concatenate(mixed, axis=1), weight, (((1,), (1,)), ((), ())), preferred_element_type=jnp.float32
    )
    return (grad_in.astype(jnp.bfloat16)[None], grad_weight)


def solution(mesh):
    devices = mesh.devices.reshape(8, 2, 4, 2, 2)
    fine = Mesh(devices, ROW + COL)
    return jax.shard_map(
        per_device,
        mesh=fine,
        in_specs=(
            P(ROW, COL, None),
            P(ROW, COL, None),
            P(COL, ROW, None),
            P(),
            P(ROW, COL, None, None, None),
            P(ROW, COL, None),
            P(ROW, COL, None),
            P(ROW, COL),
        ),
        out_specs=(P(COL, ROW, None), P()),
        check_vma=False,
    )
```

```python
import functools

import jax
import jax.numpy as jnp
from jax import lax
from jax.experimental import pallas as pl
from jax.experimental.pallas import tpu as pltpu
from jax.sharding import Mesh, PartitionSpec as P

ROW = ("z", "yh")
COL = ("x", "yl", "core")
SIDE = ("yh", "x", "yl")
GROUP = 8
CHUNKS = 2
REACH = 2


def silu_grad(grad_out, preact):
    pre_value = preact.astype(jnp.float32)
    sigmoid_val = jax.nn.sigmoid(pre_value)
    scaled = grad_out.astype(jnp.float32) * sigmoid_val * (1.0 + pre_value * (1.0 - sigmoid_val))
    return scaled.astype(jnp.bfloat16)


def tile_kernel(columns, count_ref, send_ref, row_ref, col_ref, blocks_hbm, panel_hbm, *refs):
    outs, (total, blocks_ref, panel_ref, stage, sems) = refs[:-5], refs[-5:]
    chunks = len(columns)
    _, tiles, size, width = stage.shape
    count = count_ref[0]
    loads = [pltpu.make_async_copy(blocks_hbm, blocks_ref, sems.at[0])]
    for c in range(chunks):
        loads.append(pltpu.make_async_copy(
            panel_hbm.at[:, columns[c]:columns[c] + width], panel_ref.at[c], sems.at[1 + c]
        ))
    for copy in loads:
        copy.start()
    total[...] = jnp.zeros_like(total)
    loads[0].wait()
    leaving = []
    for c in range(chunks):
        loads[1 + c].wait()

        def add_group(step, carry):
            for u in range(GROUP):
                slot = step * GROUP + u
                start = pl.multiple_of(row_ref[slot] * size, size)
                place = jnp.where(slot < count, col_ref[slot], tiles)
                total[place] += lax.dot_general(
                    blocks_ref[slot], panel_ref[c, pl.ds(start, size), :], (((0,), (0,)), ((), ())),
                    preferred_element_type=jnp.float32,
                )
            return carry

        lax.fori_loop(0, (count + GROUP - 1) // GROUP, add_group, 0)

        def store(tile, carry):
            stage[c, tile] = total[tile].astype(stage.dtype)
            if c < chunks - 1:
                total[tile] = jnp.zeros((size, width), jnp.float32)
            return carry

        lax.fori_loop(0, tiles, store, 0)
        whole, *pieces = outs[3 * c:3 * c + 3]
        first = 1 + chunks + 3 * c
        for i, ref in enumerate(pieces):
            start = send_ref[2 * c + i] * ref.shape[0]
            leaving.append(pltpu.make_async_copy(stage.at[c, pl.ds(start, ref.shape[0])], ref, sems.at[first + i]))
        leaving.append(pltpu.make_async_copy(stage.at[c], whole, sems.at[first + 2]))
        for copy in leaving[-3:]:
            copy.start()
    for copy in leaving:
        copy.wait()


def tile_sum(panel, columns, width, blocks, row_ids, col_ids, used_count, col_tiles, send):
    slots, size, _ = blocks.shape
    depth = panel.shape[0]
    chunks = len(columns)
    piece = col_tiles // lax.axis_size("z")
    hbm = pl.BlockSpec(memory_space=pl.ANY)
    outs = pl.pallas_call(
        functools.partial(tile_kernel, columns),
        out_shape=[jax.ShapeDtypeStruct((n, size, width), jnp.bfloat16) for n in (col_tiles, piece, piece)] * chunks,
        in_specs=[pl.BlockSpec(memory_space=pltpu.SMEM)] * 4 + [hbm] * 2,
        out_specs=[hbm] * (3 * chunks),
        scratch_shapes=[
            pltpu.VMEM((col_tiles + 1, size, width), jnp.float32),
            pltpu.VMEM(blocks.shape, jnp.bfloat16),
            pltpu.VMEM((chunks, depth, width), jnp.bfloat16),
            pltpu.VMEM((chunks, col_tiles, size, width), jnp.bfloat16),
            pltpu.SemaphoreType.DMA((1 + 4 * chunks,)),
        ],
        compiler_params=pltpu.CompilerParams(vmem_limit_bytes=56 * 2**20),
        cost_estimate=pl.CostEstimate(
            flops=2 * slots * size * size * width * chunks,
            bytes_accessed=2 * (blocks.size + depth * width * chunks + col_tiles * size * width * chunks),
            transcendentals=0,
        ),
    )(used_count, send, row_ids, col_ids, blocks, panel)
    return [outs[3 * c:3 * c + 3] for c in range(chunks)]


def behind(value, others):
    return lax.optimization_barrier((value, others))[0]


def shift(value, axis, way):
    size = lax.axis_size(axis)
    return lax.ppermute(value, axis, [(i, (i + way) % size) for i in range(size)])


def row_sum(partial, pieces, ways):
    size = lax.axis_size("z")
    here = lax.axis_index("z")

    def own(place):
        return lax.dynamic_index_in_dim(partial, jnp.bitwise_and(place, size - 1), 0, keepdims=False)

    arrived = []
    sent = [[] for _ in range(size // 2)]
    for moving, (way, hops) in zip(pieces, ways):
        for hop in range(hops):
            sent[hop].append(moving)
            moving = shift(moving, "z", way)
            left = hops - 1 - hop
            if left:
                moving = (moving.astype(jnp.float32) + own(here + way * left).astype(jnp.float32)).astype(jnp.bfloat16)
        arrived.append(moving)
    arrived.append(own(here))
    half = lax.axis_index("yh")

    def total(which):
        halves = [lax.dynamic_index_in_dim(t.reshape(2, -1, t.shape[-1]), which, 0, keepdims=False) for t in arrived]
        return sum(t.astype(jnp.float32) for t in halves)

    other = shift(total(1 - half).astype(jnp.bfloat16), "yh", 1)
    mixed = (total(half) + other.astype(jnp.float32)).astype(jnp.bfloat16)
    return mixed, sent


def gather_features(turned, reach):
    found = []
    for start in (turned, shift(turned, "yh", 1)):
        near = {0: start}
        for k in range(1, reach + 1):
            near[k], near[-k] = shift(near[k - 1], "z", -1), shift(near[1 - k], "z", 1)
        found.append(near)
    return found


def term_kernel(chunks, reach, place_ref, *refs):
    partials, refs = refs[:chunks], refs[chunks:]
    passing, refs = refs[:2 * chunks], refs[2 * chunks:]
    features, (out_ref, total, left, nodes, sems) = refs[:-5], refs[-5:]
    z, yh, first = place_ref[0], place_ref[1], place_ref[2]
    rows = out_ref.shape[0]
    count = 2 * reach + 1
    depth = features[0].shape[1]
    width = nodes.shape[2]
    groups = []
    used = 0
    for i in range(count):
        group = []
        for h in range(2):
            b = 2 * i + h
            at = slice(b * depth, (b + 1) * depth)
            source = features[h * count + i].at[pl.ds(pl.multiple_of(first * rows, rows), rows), :]
            group.append(pltpu.make_async_copy(source, left.at[:, at], sems.at[used]))
            used += 1
            half = pl.ds(pl.multiple_of(jnp.bitwise_xor(yh, h) * depth, depth), depth)
            for c in range(chunks):
                if abs(i - reach) == reach:
                    source = passing[2 * c + (i > reach)].at[half, :]
                else:
                    source = partials[c].at[jnp.bitwise_and(z + (i - reach), partials[c].shape[0] - 1), half, :]
                group.append(pltpu.make_async_copy(source, nodes.at[c, at, :], sems.at[used]))
                used += 1
        groups.append(group)
    for group in groups:
        for copy in group:
            copy.start()
    steps = [(0, 1), (1, 3), (3, count)]
    for step, (low, high) in enumerate(steps):
        for group in groups[low:high]:
            for copy in group:
                copy.wait()
        inner = slice(low * 2 * depth, high * 2 * depth)

        for c in range(chunks):
            columns = slice(c * width, (c + 1) * width)
            product = jnp.dot(left[:, inner], nodes[c, inner, :], preferred_element_type=jnp.float32)
            if step:
                product = total[:, columns] + product
            if step < len(steps) - 1:
                total[:, columns] = product
            else:
                out_ref[:, columns] = product.astype(out_ref.dtype)


def weight_terms(features, partials, passing, reach, place):
    distances = list(range(-reach, reach + 1))
    features = [near[k] for near in features for k in distances]
    height, depth = features[0].shape
    width = partials[0].shape[2]
    chunks = len(partials)
    blocks = len(features)
    operands = list(partials) + [p for pair in passing for p in pair] + features
    return pl.pallas_call(
        functools.partial(term_kernel, chunks, reach),
        out_shape=jax.ShapeDtypeStruct((height // 2, chunks * width), jnp.bfloat16),
        in_specs=[pl.BlockSpec(memory_space=pltpu.SMEM)] + [pl.BlockSpec(memory_space=pl.ANY)] * len(operands),
        out_specs=pl.BlockSpec(memory_space=pltpu.VMEM),
        scratch_shapes=[
            pltpu.VMEM((height // 2, chunks * width), jnp.float32),
            pltpu.VMEM((height // 2, blocks * depth), jnp.bfloat16),
            pltpu.VMEM((chunks, blocks * depth, width), jnp.bfloat16),
            pltpu.SemaphoreType.DMA(((1 + chunks) * blocks,)),
        ],
        compiler_params=pltpu.CompilerParams(vmem_limit_bytes=56 * 2**20),
        cost_estimate=pl.CostEstimate(
            flops=height * blocks * depth * chunks * width,
            bytes_accessed=2 * blocks * depth * (height // 2 + chunks * width) + height * chunks * width,
            transcendentals=0,
        ),
    )(place, *operands)


def place_kernel(which_ref, half_ref, *refs):
    out_hbm, stage, sem = refs[-3:]
    rows = stage.shape[0]
    stage[...] = half_ref[...].astype(stage.dtype)
    copy = pltpu.make_async_copy(stage, out_hbm.at[pl.ds(pl.multiple_of(which_ref[0] * rows, rows), rows), :], sem)
    copy.start()
    copy.wait()


def place_half(half, which, whole=()):
    rows, width = half.shape
    whole = [whole] if len(whole) else []
    hbm = pl.BlockSpec(memory_space=pl.ANY)
    return pl.pallas_call(
        place_kernel,
        out_shape=jax.ShapeDtypeStruct((2 * rows, width), jnp.float32),
        in_specs=[pl.BlockSpec(memory_space=pltpu.SMEM), pl.BlockSpec(memory_space=pltpu.VMEM)] + [hbm] * len(whole),
        out_specs=hbm,
        scratch_shapes=[pltpu.VMEM((rows, width), jnp.float32), pltpu.SemaphoreType.DMA],
        input_output_aliases={2: 0} if whole else {},
    )(which.reshape(1), half, *whole)


def sum_everywhere(mine, other, second, third):
    side = lax.axis_size(SIDE)
    depth = lax.axis_size("z")
    core = lax.axis_index("core")
    part = mine.astype(jnp.float32) + shift(other, "core", 1).astype(jnp.float32)
    part = part.astype(jnp.bfloat16).reshape(side, -1, part.shape[-1])
    part = lax.all_to_all(part, SIDE, 0, 0, tiled=True)
    part = jnp.sum(part.astype(jnp.float32), axis=0).astype(jnp.bfloat16)
    part = behind(part, second)
    part = lax.all_to_all(jnp.broadcast_to(part[None], (depth,) + part.shape), "z", 0, 0, tiled=True)
    part = jnp.sum(part.astype(jnp.float32), axis=0).astype(jnp.bfloat16)
    part = behind(part, third)
    half = lax.all_to_all(jnp.broadcast_to(part[None], (side,) + part.shape), SIDE, 0, 0, tiled=True)
    half = half.reshape(-1, half.shape[-1])
    return place_half(shift(half, "core", 1), 1 - core, place_half(half, core))


def per_device(grad_out, preact, features, weight, tile_values, tile_row, tile_col, tile_count):
    size = tile_values.shape[-1]
    width = grad_out.shape[-1] // CHUNKS
    col_tiles = features.shape[1] * lax.axis_size(ROW) // size
    tiles = (tile_values[0, 0], tile_row[0, 0], tile_col[0, 0], tile_count[0], col_tiles)
    z, depth = lax.axis_index("z"), lax.axis_size("z")

    panel = lax.all_gather(silu_grad(grad_out[0], preact[0]), COL, axis=0, tiled=True)
    near = gather_features(features[0].T, REACH)
    ways = (((1, 4), (-1, 3)), ((1, 3), (-1, 4)))
    before = [near_by[k] for near_by in near for k in (REACH, -REACH)]
    partials = []
    passing = []
    mixed = []
    sent = [[] for _ in range(depth // 2)]
    send = jnp.stack([jnp.bitwise_and(z + way * hops, depth - 1) for pair in ways for way, hops in pair])
    columns = tuple(c * width for c in range(CHUNKS))
    chunks = tile_sum(panel, columns, width, *tiles, behind(send, before))
    for (whole, *pieces), pair in zip(chunks, ways):
        partials.append(whole.reshape(depth, -1, width))
        total, moves = row_sum(partials[-1], [p.reshape(-1, width) for p in pieces], pair)
        mixed.append(total)
        for hop, sums in enumerate(moves):
            sent[hop] += sums
        far = {way: moves[hops - REACH][i] for i, (way, hops) in enumerate(pair)}
        passing.append((far[-1], far[1]))
    core = lax.axis_index("core")
    theirs, ours = [jnp.stack([z, lax.axis_index("yh"), half]) for half in (1 - core, core)]
    theirs = weight_terms(near, partials, passing, REACH, theirs)
    ours = weight_terms(near, partials, passing, REACH, behind(ours, theirs))
    grad_weight = sum_everywhere(ours, theirs, sent[3], mixed)
    grad_in = lax.dot_general(
        jnp.concatenate(mixed, axis=1), weight, (((1,), (1,)), ((), ())), preferred_element_type=jnp.float32
    )
    return (grad_in.astype(jnp.bfloat16)[None], grad_weight)


def solution(mesh):
    devices = mesh.devices.reshape(8, 2, 4, 2, 2)
    fine = Mesh(devices, ROW + COL)
    return jax.shard_map(
        per_device,
        mesh=fine,
        in_specs=(
            P(ROW, COL, None),
            P(ROW, COL, None),
            P(COL, ROW, None),
            P(),
            P(ROW, COL, None, None, None),
            P(ROW, COL, None),
            P(ROW, COL, None),
            P(ROW, COL),
        ),
        out_specs=(P(COL, ROW, None), P()),
        check_vma=False,
    )
```

```python
import functools

import jax
import jax.numpy as jnp
from jax import lax
from jax.experimental import pallas as pl
from jax.experimental.pallas import tpu as pltpu
from jax.sharding import Mesh, PartitionSpec as P

ROW = ("z", "yh")
COL = ("x", "yl", "core")
SIDE = ("yh", "x", "yl")
GROUP = 8
CHUNKS = 2
REACH = 2


def silu_grad(grad_out, preact):
    pre_value = preact.astype(jnp.float32)
    sigmoid_val = jax.nn.sigmoid(pre_value)
    scaled = grad_out.astype(jnp.float32) * sigmoid_val * (1.0 + pre_value * (1.0 - sigmoid_val))
    return scaled.astype(jnp.bfloat16)


def tile_kernel(columns, count_ref, send_ref, row_ref, col_ref, blocks_hbm, panel_hbm, *refs):
    outs, (total, blocks_ref, panel_ref, stage, sems) = refs[:-5], refs[-5:]
    chunks = len(columns)
    _, tiles, size, width = stage.shape
    count = count_ref[0]
    loads = [pltpu.make_async_copy(blocks_hbm, blocks_ref, sems.at[0])]
    for c in range(chunks):
        loads.append(pltpu.make_async_copy(
            panel_hbm.at[:, columns[c]:columns[c] + width], panel_ref.at[c], sems.at[1 + c]
        ))
    for copy in loads[:2]:
        copy.start()
    total[...] = jnp.zeros_like(total)
    loads[0].wait()
    leaving = []
    for c in range(chunks):
        loads[1 + c].wait()
        for copy in loads[2 + c:3 + c]:
            copy.start()

        def add_group(step, carry):
            for u in range(GROUP):
                slot = step * GROUP + u
                start = pl.multiple_of(row_ref[slot] * size, size)
                place = jnp.where(slot < count, col_ref[slot], tiles)
                total[place] += lax.dot_general(
                    blocks_ref[slot], panel_ref[c, pl.ds(start, size), :], (((0,), (0,)), ((), ())),
                    preferred_element_type=jnp.float32,
                )
            return carry

        lax.fori_loop(0, (count + GROUP - 1) // GROUP, add_group, 0)

        def store(tile, carry):
            stage[c, tile] = total[tile].astype(stage.dtype)
            if c < chunks - 1:
                total[tile] = jnp.zeros((size, width), jnp.float32)
            return carry

        whole, *pieces = outs[3 * c:3 * c + 3]
        depth = pieces[0].shape[0]
        parts = tiles // depth
        first = 1 + chunks + (parts + 2) * c
        for i in range(parts):
            at = pl.ds(i * depth, depth)
            lax.fori_loop(i * depth, (i + 1) * depth, store, 0)
            leaving.append(pltpu.make_async_copy(stage.at[c, at], whole.at[at], sems.at[first + i]))
            leaving[-1].start()
        for i, ref in enumerate(pieces):
            at = pl.ds(send_ref[2 * c + i] * depth, depth)
            leaving.append(pltpu.make_async_copy(stage.at[c, at], ref, sems.at[first + parts + i]))
            leaving[-1].start()
    for copy in leaving:
        copy.wait()


def tile_sum(panel, columns, width, blocks, row_ids, col_ids, used_count, col_tiles, send):
    slots, size, _ = blocks.shape
    depth = panel.shape[0]
    chunks = len(columns)
    piece = col_tiles // lax.axis_size("z")
    hbm = pl.BlockSpec(memory_space=pl.ANY)
    outs = pl.pallas_call(
        functools.partial(tile_kernel, columns),
        out_shape=[jax.ShapeDtypeStruct((n, size, width), jnp.bfloat16) for n in (col_tiles, piece, piece)] * chunks,
        in_specs=[pl.BlockSpec(memory_space=pltpu.SMEM)] * 4 + [hbm] * 2,
        out_specs=[hbm] * (3 * chunks),
        scratch_shapes=[
            pltpu.VMEM((col_tiles + 1, size, width), jnp.float32),
            pltpu.VMEM(blocks.shape, jnp.bfloat16),
            pltpu.VMEM((chunks, depth, width), jnp.bfloat16),
            pltpu.VMEM((chunks, col_tiles, size, width), jnp.bfloat16),
            pltpu.SemaphoreType.DMA((1 + chunks + (col_tiles // piece + 2) * chunks,)),
        ],
        compiler_params=pltpu.CompilerParams(vmem_limit_bytes=56 * 2**20),
        cost_estimate=pl.CostEstimate(
            flops=2 * slots * size * size * width * chunks,
            bytes_accessed=2 * (blocks.size + depth * width * chunks + col_tiles * size * width * chunks),
            transcendentals=0,
        ),
    )(used_count, send, row_ids, col_ids, blocks, panel)
    return [outs[3 * c:3 * c + 3] for c in range(chunks)]


def behind(value, others):
    return lax.optimization_barrier((value, others))[0]


def shift(value, axis, way):
    size = lax.axis_size(axis)
    return lax.ppermute(value, axis, [(i, (i + way) % size) for i in range(size)])


def row_chains(partial, pieces, ways):
    size = lax.axis_size("z")
    here = lax.axis_index("z")
    arrived = []
    sent = [[] for _ in range(size // 2)]
    for moving, (way, hops) in zip(pieces, ways):
        for hop in range(hops):
            sent[hop].append(moving)
            moving = shift(moving, "z", way)
            left = hops - 1 - hop
            if left:
                place = jnp.bitwise_and(here + way * left, size - 1)
                own = lax.dynamic_index_in_dim(partial, place, 0, keepdims=False)
                moving = (moving.astype(jnp.float32) + own.astype(jnp.float32)).astype(jnp.bfloat16)
        arrived.append(moving)
    return arrived, sent


def row_sum(partials, arrived):
    here = lax.axis_index("z")
    half = lax.axis_index("yh")

    def total(which):
        sums = []
        for partial, terms in zip(partials, arrived):
            width = partial.shape[-1]
            own = partial.reshape(2 * partial.shape[0], -1, width)
            parts = [lax.dynamic_index_in_dim(own, 2 * here + which, 0, keepdims=False)]
            parts += [lax.dynamic_index_in_dim(t.reshape(2, -1, width), which, 0, keepdims=False) for t in terms]
            sums.append(sum(p.astype(jnp.float32) for p in parts))
        return jnp.concatenate(sums, axis=1)

    other = shift(total(1 - half).astype(jnp.bfloat16), "yh", 1)
    return (total(half) + other.astype(jnp.float32)).astype(jnp.bfloat16)


def gather_features(turned, reach):
    found = []
    for start in (turned, shift(turned, "yh", 1)):
        near = {0: start}
        for k in range(1, reach + 1):
            near[k], near[-k] = shift(near[k - 1], "z", -1), shift(near[1 - k], "z", 1)
        found.append(near)
    return found


def term_kernel(chunks, reach, place_ref, *refs):
    partials, refs = refs[:chunks], refs[chunks:]
    passing, refs = refs[:2 * chunks], refs[2 * chunks:]
    features, (out_ref, total, left, nodes, sems) = refs[:-5], refs[-5:]
    z, yh, first = place_ref[0], place_ref[1], place_ref[2]
    rows = out_ref.shape[0]
    count = 2 * reach + 1
    depth = features[0].shape[1]
    width = nodes.shape[2]
    groups = []
    used = 0
    for i in range(count):
        group = []
        for h in range(2):
            b = 2 * i + h
            at = slice(b * depth, (b + 1) * depth)
            source = features[h * count + i].at[pl.ds(pl.multiple_of(first * rows, rows), rows), :]
            group.append(pltpu.make_async_copy(source, left.at[:, at], sems.at[used]))
            used += 1
            half = pl.ds(pl.multiple_of(jnp.bitwise_xor(yh, h) * depth, depth), depth)
            for c in range(chunks):
                if abs(i - reach) == reach:
                    source = passing[2 * c + (i > reach)].at[half, :]
                else:
                    source = partials[c].at[jnp.bitwise_and(z + (i - reach), partials[c].shape[0] - 1), half, :]
                group.append(pltpu.make_async_copy(source, nodes.at[c, at, :], sems.at[used]))
                used += 1
        groups.append(group)
    for group in groups:
        for copy in group:
            copy.start()
    steps = [(0, 1), (1, 3), (3, count)]
    for step, (low, high) in enumerate(steps):
        for group in groups[low:high]:
            for copy in group:
                copy.wait()
        inner = slice(low * 2 * depth, high * 2 * depth)

        for c in range(chunks):
            columns = slice(c * width, (c + 1) * width)
            product = jnp.dot(left[:, inner], nodes[c, inner, :], preferred_element_type=jnp.float32)
            if step:
                product = total[:, columns] + product
            if step < len(steps) - 1:
                total[:, columns] = product
            else:
                out_ref[:, columns] = product.astype(out_ref.dtype)


def weight_terms(features, partials, passing, reach, place):
    distances = list(range(-reach, reach + 1))
    features = [near[k] for near in features for k in distances]
    height, depth = features[0].shape
    width = partials[0].shape[2]
    chunks = len(partials)
    blocks = len(features)
    operands = list(partials) + [p for pair in passing for p in pair] + features
    return pl.pallas_call(
        functools.partial(term_kernel, chunks, reach),
        out_shape=jax.ShapeDtypeStruct((height // 2, chunks * width), jnp.bfloat16),
        in_specs=[pl.BlockSpec(memory_space=pltpu.SMEM)] + [pl.BlockSpec(memory_space=pl.ANY)] * len(operands),
        out_specs=pl.BlockSpec(memory_space=pltpu.VMEM),
        scratch_shapes=[
            pltpu.VMEM((height // 2, chunks * width), jnp.float32),
            pltpu.VMEM((height // 2, blocks * depth), jnp.bfloat16),
            pltpu.VMEM((chunks, blocks * depth, width), jnp.bfloat16),
            pltpu.SemaphoreType.DMA(((1 + chunks) * blocks,)),
        ],
        compiler_params=pltpu.CompilerParams(vmem_limit_bytes=56 * 2**20),
        cost_estimate=pl.CostEstimate(
            flops=height * blocks * depth * chunks * width,
            bytes_accessed=2 * blocks * depth * (height // 2 + chunks * width) + height * chunks * width,
            transcendentals=0,
        ),
    )(place, *operands)


def place_kernel(which_ref, half_ref, *refs):
    out_hbm, stage, sem = refs[-3:]
    rows = stage.shape[0]
    stage[...] = half_ref[...].astype(stage.dtype)
    copy = pltpu.make_async_copy(stage, out_hbm.at[pl.ds(pl.multiple_of(which_ref[0] * rows, rows), rows), :], sem)
    copy.start()
    copy.wait()


def place_half(half, which, whole=()):
    rows, width = half.shape
    whole = [whole] if len(whole) else []
    hbm = pl.BlockSpec(memory_space=pl.ANY)
    return pl.pallas_call(
        place_kernel,
        out_shape=jax.ShapeDtypeStruct((2 * rows, width), jnp.float32),
        in_specs=[pl.BlockSpec(memory_space=pltpu.SMEM), pl.BlockSpec(memory_space=pltpu.VMEM)] + [hbm] * len(whole),
        out_specs=hbm,
        scratch_shapes=[pltpu.VMEM((rows, width), jnp.float32), pltpu.SemaphoreType.DMA],
        input_output_aliases={2: 0} if whole else {},
    )(which.reshape(1), half, *whole)


def sum_everywhere(mine, other, second):
    side = lax.axis_size(SIDE)
    depth = lax.axis_size("z")
    core = lax.axis_index("core")
    part = mine.astype(jnp.float32) + shift(other, "core", 1).astype(jnp.float32)
    part = part.astype(jnp.bfloat16).reshape(side, -1, part.shape[-1])
    part = lax.all_to_all(part, SIDE, 0, 0, tiled=True)
    part = jnp.sum(part.astype(jnp.float32), axis=0).astype(jnp.bfloat16)
    part = behind(part, second)
    part = lax.all_to_all(jnp.broadcast_to(part[None], (depth,) + part.shape), "z", 0, 0, tiled=True)
    part = jnp.sum(part.astype(jnp.float32), axis=0).astype(jnp.bfloat16)
    half = lax.all_to_all(jnp.broadcast_to(part[None], (side,) + part.shape), SIDE, 0, 0, tiled=True)
    half = half.reshape(-1, half.shape[-1])
    return place_half(shift(half, "core", 1), 1 - core, place_half(half, core))


def per_device(grad_out, preact, features, weight, tile_values, tile_row, tile_col, tile_count):
    size = tile_values.shape[-1]
    width = grad_out.shape[-1] // CHUNKS
    col_tiles = features.shape[1] * lax.axis_size(ROW) // size
    tiles = (tile_values[0, 0], tile_row[0, 0], tile_col[0, 0], tile_count[0], col_tiles)
    z, depth = lax.axis_index("z"), lax.axis_size("z")

    panel = lax.all_gather(silu_grad(grad_out[0], preact[0]), COL, axis=0, tiled=True)
    near = gather_features(features[0].T, REACH)
    ways = (((1, 4), (-1, 3)), ((1, 3), (-1, 4)))
    before = [near_by[k] for near_by in near for k in (REACH, -REACH)]
    partials = []
    passing = []
    arrived = []
    sent = [[] for _ in range(depth // 2)]
    send = jnp.stack([jnp.bitwise_and(z + way * hops, depth - 1) for pair in ways for way, hops in pair])
    columns = tuple(c * width for c in range(CHUNKS))
    chunks = tile_sum(panel, columns, width, *tiles, behind(send, before))
    for (whole, *pieces), pair in zip(chunks, ways):
        partials.append(whole.reshape(depth, -1, width))
        ends, moves = row_chains(partials[-1], [p.reshape(-1, width) for p in pieces], pair)
        arrived.append(ends)
        for hop, sums in enumerate(moves):
            sent[hop] += sums
        far = {way: moves[hops - REACH][i] for i, (way, hops) in enumerate(pair)}
        passing.append((far[-1], far[1]))
    core = lax.axis_index("core")
    theirs, ours = [jnp.stack([z, lax.axis_index("yh"), half]) for half in (1 - core, core)]
    theirs = weight_terms(near, partials, passing, REACH, theirs)
    ours = weight_terms(near, partials, passing, REACH, behind(ours, theirs))
    grad_weight = sum_everywhere(ours, theirs, sent[3])
    mixed = row_sum(partials, arrived)
    grad_in = lax.dot_general(
        mixed, weight, (((1,), (1,)), ((), ())), preferred_element_type=jnp.float32
    )
    return (grad_in.astype(jnp.bfloat16)[None], grad_weight)


def solution(mesh):
    devices = mesh.devices.reshape(8, 2, 4, 2, 2)
    fine = Mesh(devices, ROW + COL)
    return jax.shard_map(
        per_device,
        mesh=fine,
        in_specs=(
            P(ROW, COL, None),
            P(ROW, COL, None),
            P(COL, ROW, None),
            P(),
            P(ROW, COL, None, None, None),
            P(ROW, COL, None),
            P(ROW, COL, None),
            P(ROW, COL),
        ),
        out_specs=(P(COL, ROW, None), P()),
        check_vma=False,
    )
```

```python
import functools

import jax
import jax.numpy as jnp
from jax import lax
from jax.experimental import pallas as pl
from jax.experimental.pallas import tpu as pltpu
from jax.sharding import Mesh, PartitionSpec as P

ROW = ("z", "yh")
COL = ("x", "yl", "core")
SIDE = ("yh", "x", "yl")
GROUP = 8
CHUNKS = 2
REACH = 2


def silu_grad(grad_out, preact):
    pre_value = preact.astype(jnp.float32)
    sigmoid_val = jax.nn.sigmoid(pre_value)
    scaled = grad_out.astype(jnp.float32) * sigmoid_val * (1.0 + pre_value * (1.0 - sigmoid_val))
    return scaled.astype(jnp.bfloat16)


def tile_kernel(columns, count_ref, send_ref, row_ref, col_ref, blocks_hbm, panel_hbm, *refs):
    outs, (total, blocks_ref, panel_ref, stage, sems) = refs[:-5], refs[-5:]
    chunks = len(columns)
    _, tiles, size, width = stage.shape
    count = count_ref[0]
    loads = [pltpu.make_async_copy(blocks_hbm, blocks_ref, sems.at[0])]
    for c in range(chunks):
        loads.append(pltpu.make_async_copy(
            panel_hbm.at[:, columns[c]:columns[c] + width], panel_ref.at[c], sems.at[1 + c]
        ))
    for copy in loads[:2]:
        copy.start()
    total[...] = jnp.zeros_like(total)
    loads[0].wait()
    leaving = []
    for c in range(chunks):
        loads[1 + c].wait()
        for copy in loads[2 + c:3 + c]:
            copy.start()

        def add_group(step, carry):
            for u in range(GROUP):
                slot = step * GROUP + u
                start = pl.multiple_of(row_ref[slot] * size, size)
                place = jnp.where(slot < count, col_ref[slot], tiles)
                total[place] += lax.dot_general(
                    blocks_ref[slot], panel_ref[c, pl.ds(start, size), :], (((0,), (0,)), ((), ())),
                    preferred_element_type=jnp.float32,
                )
            return carry

        lax.fori_loop(0, (count + GROUP - 1) // GROUP, add_group, 0)

        def store(tile, carry):
            stage[c, tile] = total[tile].astype(stage.dtype)
            if c < chunks - 1:
                total[tile] = jnp.zeros((size, width), jnp.float32)
            return carry

        whole, *pieces = outs[3 * c:3 * c + 3]
        depth = pieces[0].shape[0]
        parts = tiles // depth
        first = 1 + chunks + (parts + 2) * c
        for i in range(parts):
            at = pl.ds(i * depth, depth)
            lax.fori_loop(i * depth, (i + 1) * depth, store, 0)
            leaving.append(pltpu.make_async_copy(stage.at[c, at], whole.at[at], sems.at[first + i]))
            leaving[-1].start()
        for i, ref in enumerate(pieces):
            at = pl.ds(send_ref[2 * c + i] * depth, depth)
            leaving.append(pltpu.make_async_copy(stage.at[c, at], ref, sems.at[first + parts + i]))
            leaving[-1].start()
    for copy in leaving:
        copy.wait()


def tile_sum(panel, columns, width, blocks, row_ids, col_ids, used_count, col_tiles, send):
    slots, size, _ = blocks.shape
    depth = panel.shape[0]
    chunks = len(columns)
    piece = col_tiles // lax.axis_size("z")
    hbm = pl.BlockSpec(memory_space=pl.ANY)
    outs = pl.pallas_call(
        functools.partial(tile_kernel, columns),
        out_shape=[jax.ShapeDtypeStruct((n, size, width), jnp.bfloat16) for n in (col_tiles, piece, piece)] * chunks,
        in_specs=[pl.BlockSpec(memory_space=pltpu.SMEM)] * 4 + [hbm] * 2,
        out_specs=[hbm] * (3 * chunks),
        scratch_shapes=[
            pltpu.VMEM((col_tiles + 1, size, width), jnp.float32),
            pltpu.VMEM(blocks.shape, jnp.bfloat16),
            pltpu.VMEM((chunks, depth, width), jnp.bfloat16),
            pltpu.VMEM((chunks, col_tiles, size, width), jnp.bfloat16),
            pltpu.SemaphoreType.DMA((1 + chunks + (col_tiles // piece + 2) * chunks,)),
        ],
        compiler_params=pltpu.CompilerParams(vmem_limit_bytes=56 * 2**20),
        cost_estimate=pl.CostEstimate(
            flops=2 * slots * size * size * width * chunks,
            bytes_accessed=2 * (blocks.size + depth * width * chunks + col_tiles * size * width * chunks),
            transcendentals=0,
        ),
    )(used_count, send, row_ids, col_ids, blocks, panel)
    return [outs[3 * c:3 * c + 3] for c in range(chunks)]


def behind(value, others):
    return lax.optimization_barrier((value, others))[0]


def shift(value, axis, way):
    size = lax.axis_size(axis)
    return lax.ppermute(value, axis, [(i, (i + way) % size) for i in range(size)])


def row_chains(partial, pieces, ways):
    size = lax.axis_size("z")
    here = lax.axis_index("z")
    arrived = []
    sent = [[] for _ in range(size // 2)]
    for moving, (way, hops) in zip(pieces, ways):
        for hop in range(hops):
            sent[hop].append(moving)
            moving = shift(moving, "z", way)
            left = hops - 1 - hop
            if left:
                place = jnp.bitwise_and(here + way * left, size - 1)
                own = lax.dynamic_index_in_dim(partial, place, 0, keepdims=False)
                moving = (moving.astype(jnp.float32) + own.astype(jnp.float32)).astype(jnp.bfloat16)
        arrived.append(moving)
    return arrived, sent


def row_sum(partials, arrived):
    here = lax.axis_index("z")
    half = lax.axis_index("yh")

    def total(which):
        sums = []
        for partial, terms in zip(partials, arrived):
            width = partial.shape[-1]
            own = partial.reshape(2 * partial.shape[0], -1, width)
            parts = [lax.dynamic_index_in_dim(own, 2 * here + which, 0, keepdims=False)]
            parts += [lax.dynamic_index_in_dim(t.reshape(2, -1, width), which, 0, keepdims=False) for t in terms]
            sums.append(sum(p.astype(jnp.float32) for p in parts))
        return jnp.concatenate(sums, axis=1)

    other = shift(total(1 - half).astype(jnp.bfloat16), "yh", 1)
    return (total(half) + other.astype(jnp.float32)).astype(jnp.bfloat16)


def gather_features(turned, reach):
    found = []
    for start in (turned, shift(turned, "yh", 1)):
        near = {0: start}
        for k in range(1, reach + 1):
            near[k], near[-k] = shift(near[k - 1], "z", -1), shift(near[1 - k], "z", 1)
        found.append(near)
    return found


def term_kernel(chunks, reach, place_ref, *refs):
    partials, refs = refs[:chunks], refs[chunks:]
    passing, refs = refs[:2 * chunks], refs[2 * chunks:]
    features, (out_ref, total, left, nodes, sems) = refs[:-5], refs[-5:]
    z, yh, first = place_ref[0], place_ref[1], place_ref[2]
    rows = out_ref.shape[0]
    count = 2 * reach + 1
    depth = features[0].shape[1]
    width = nodes.shape[2]
    groups = []
    used = 0
    for i in range(count):
        group = []
        for h in range(2):
            b = 2 * i + h
            at = slice(b * depth, (b + 1) * depth)
            source = features[h * count + i].at[pl.ds(pl.multiple_of(first * rows, rows), rows), :]
            group.append(pltpu.make_async_copy(source, left.at[:, at], sems.at[used]))
            used += 1
            half = pl.ds(pl.multiple_of(jnp.bitwise_xor(yh, h) * depth, depth), depth)
            for c in range(chunks):
                if abs(i - reach) == reach:
                    source = passing[2 * c + (i > reach)].at[half, :]
                else:
                    source = partials[c].at[jnp.bitwise_and(z + (i - reach), partials[c].shape[0] - 1), half, :]
                group.append(pltpu.make_async_copy(source, nodes.at[c, at, :], sems.at[used]))
                used += 1
        groups.append(group)
    for group in groups:
        for copy in group:
            copy.start()
    steps = [(0, 1), (1, 3), (3, count)]
    for step, (low, high) in enumerate(steps):
        for group in groups[low:high]:
            for copy in group:
                copy.wait()
        inner = slice(low * 2 * depth, high * 2 * depth)

        for c in range(chunks):
            columns = slice(c * width, (c + 1) * width)
            product = jnp.dot(left[:, inner], nodes[c, inner, :], preferred_element_type=jnp.float32)
            if step:
                product = total[:, columns] + product
            if step < len(steps) - 1:
                total[:, columns] = product
            else:
                out_ref[:, columns] = product.astype(out_ref.dtype)


def weight_terms(features, partials, passing, reach, place):
    distances = list(range(-reach, reach + 1))
    features = [near[k] for near in features for k in distances]
    height, depth = features[0].shape
    width = partials[0].shape[2]
    chunks = len(partials)
    blocks = len(features)
    operands = list(partials) + [p for pair in passing for p in pair] + features
    return pl.pallas_call(
        functools.partial(term_kernel, chunks, reach),
        out_shape=jax.ShapeDtypeStruct((height // 2, chunks * width), jnp.bfloat16),
        in_specs=[pl.BlockSpec(memory_space=pltpu.SMEM)] + [pl.BlockSpec(memory_space=pl.ANY)] * len(operands),
        out_specs=pl.BlockSpec(memory_space=pltpu.VMEM),
        scratch_shapes=[
            pltpu.VMEM((height // 2, chunks * width), jnp.float32),
            pltpu.VMEM((height // 2, blocks * depth), jnp.bfloat16),
            pltpu.VMEM((chunks, blocks * depth, width), jnp.bfloat16),
            pltpu.SemaphoreType.DMA(((1 + chunks) * blocks,)),
        ],
        compiler_params=pltpu.CompilerParams(vmem_limit_bytes=56 * 2**20),
        cost_estimate=pl.CostEstimate(
            flops=height * blocks * depth * chunks * width,
            bytes_accessed=2 * blocks * depth * (height // 2 + chunks * width) + height * chunks * width,
            transcendentals=0,
        ),
    )(place, *operands)


def place_kernel(which_ref, half_ref, *refs):
    out_hbm, stage, sem = refs[-3:]
    rows = stage.shape[0]
    stage[...] = half_ref[...].astype(stage.dtype)
    copy = pltpu.make_async_copy(stage, out_hbm.at[pl.ds(pl.multiple_of(which_ref[0] * rows, rows), rows), :], sem)
    copy.start()
    copy.wait()


def place_half(half, which, whole=()):
    rows, width = half.shape
    whole = [whole] if len(whole) else []
    hbm = pl.BlockSpec(memory_space=pl.ANY)
    return pl.pallas_call(
        place_kernel,
        out_shape=jax.ShapeDtypeStruct((2 * rows, width), jnp.float32),
        in_specs=[pl.BlockSpec(memory_space=pltpu.SMEM), pl.BlockSpec(memory_space=pltpu.VMEM)] + [hbm] * len(whole),
        out_specs=hbm,
        scratch_shapes=[pltpu.VMEM((rows, width), jnp.float32), pltpu.SemaphoreType.DMA],
        input_output_aliases={2: 0} if whole else {},
    )(which.reshape(1), half, *whole)


def sum_everywhere(mine, other, second, third):
    side = lax.axis_size(SIDE)
    depth = lax.axis_size("z")
    core = lax.axis_index("core")
    part = mine.astype(jnp.float32) + shift(other, "core", 1).astype(jnp.float32)
    part = part.astype(jnp.bfloat16).reshape(side, -1, part.shape[-1])
    part = lax.all_to_all(part, SIDE, 0, 0, tiled=True)
    part = jnp.sum(part.astype(jnp.float32), axis=0).astype(jnp.bfloat16)
    part = behind(part, second)
    part = lax.all_to_all(jnp.broadcast_to(part[None], (depth,) + part.shape), "z", 0, 0, tiled=True)
    part = jnp.sum(part.astype(jnp.float32), axis=0).astype(jnp.bfloat16)
    part = behind(part, third)
    half = lax.all_to_all(jnp.broadcast_to(part[None], (side,) + part.shape), SIDE, 0, 0, tiled=True)
    half = half.reshape(-1, half.shape[-1])
    return place_half(shift(half, "core", 1), 1 - core, place_half(half, core))


def per_device(grad_out, preact, features, weight, tile_values, tile_row, tile_col, tile_count):
    size = tile_values.shape[-1]
    width = grad_out.shape[-1] // CHUNKS
    col_tiles = features.shape[1] * lax.axis_size(ROW) // size
    tiles = (tile_values[0, 0], tile_row[0, 0], tile_col[0, 0], tile_count[0], col_tiles)
    z, depth = lax.axis_index("z"), lax.axis_size("z")

    panel = lax.all_gather(silu_grad(grad_out[0], preact[0]), COL, axis=0, tiled=True)
    near = gather_features(features[0].T, REACH)
    ways = (((1, 4), (-1, 3)), ((1, 3), (-1, 4)))
    before = [near_by[k] for near_by in near for k in (REACH, -REACH)]
    partials = []
    passing = []
    arrived = []
    sent = [[] for _ in range(depth // 2)]
    send = jnp.stack([jnp.bitwise_and(z + way * hops, depth - 1) for pair in ways for way, hops in pair])
    columns = tuple(c * width for c in range(CHUNKS))
    chunks = tile_sum(panel, columns, width, *tiles, behind(send, before))
    for (whole, *pieces), pair in zip(chunks, ways):
        partials.append(whole.reshape(depth, -1, width))
        ends, moves = row_chains(partials[-1], [p.reshape(-1, width) for p in pieces], pair)
        arrived.append(ends)
        for hop, sums in enumerate(moves):
            sent[hop] += sums
        far = {way: moves[hops - REACH][i] for i, (way, hops) in enumerate(pair)}
        passing.append((far[-1], far[1]))
    core = lax.axis_index("core")
    theirs, ours = [jnp.stack([z, lax.axis_index("yh"), half]) for half in (1 - core, core)]
    theirs = weight_terms(near, partials, passing, REACH, theirs)
    ours = weight_terms(near, partials, passing, REACH, behind(ours, theirs))
    grad_weight = sum_everywhere(ours, theirs, sent[3], arrived)
    mixed = row_sum(partials, arrived)
    grad_in = lax.dot_general(
        mixed, weight, (((1,), (1,)), ((), ())), preferred_element_type=jnp.float32
    )
    return (grad_in.astype(jnp.bfloat16)[None], grad_weight)


def solution(mesh):
    devices = mesh.devices.reshape(8, 2, 4, 2, 2)
    fine = Mesh(devices, ROW + COL)
    return jax.shard_map(
        per_device,
        mesh=fine,
        in_specs=(
            P(ROW, COL, None),
            P(ROW, COL, None),
            P(COL, ROW, None),
            P(),
            P(ROW, COL, None, None, None),
            P(ROW, COL, None),
            P(ROW, COL, None),
            P(ROW, COL),
        ),
        out_specs=(P(COL, ROW, None), P()),
        check_vma=False,
    )
```

```python
import functools

import jax
import jax.numpy as jnp
from jax import lax
from jax.experimental import pallas as pl
from jax.experimental.pallas import tpu as pltpu
from jax.sharding import Mesh, PartitionSpec as P

ROW = ("z", "yh")
COL = ("x", "yl", "core")
SIDE = ("yh", "x", "yl")
GROUP = 8
CHUNKS = 2
REACH = 2


def silu_grad(grad_out, preact):
    pre_value = preact.astype(jnp.float32)
    sigmoid_val = jax.nn.sigmoid(pre_value)
    scaled = grad_out.astype(jnp.float32) * sigmoid_val * (1.0 + pre_value * (1.0 - sigmoid_val))
    return scaled.astype(jnp.bfloat16)


def tile_kernel(columns, count_ref, send_ref, row_ref, col_ref, blocks_hbm, panel_hbm, *refs):
    outs, (total, blocks_ref, panel_ref, stage, sems) = refs[:-5], refs[-5:]
    chunks = len(columns)
    _, tiles, size, width = stage.shape
    count = count_ref[0]
    loads = [pltpu.make_async_copy(blocks_hbm, blocks_ref, sems.at[0])]
    for c in range(chunks):
        loads.append(pltpu.make_async_copy(
            panel_hbm.at[:, columns[c]:columns[c] + width], panel_ref.at[c], sems.at[1 + c]
        ))
    for copy in loads[:2]:
        copy.start()
    total[...] = jnp.zeros_like(total)
    loads[0].wait()
    leaving = []
    for c in range(chunks):
        loads[1 + c].wait()
        for copy in loads[2 + c:3 + c]:
            copy.start()

        def add_group(step, carry):
            for u in range(GROUP):
                slot = step * GROUP + u
                start = pl.multiple_of(row_ref[slot] * size, size)
                place = jnp.where(slot < count, col_ref[slot], tiles)
                total[place] += lax.dot_general(
                    blocks_ref[slot], panel_ref[c, pl.ds(start, size), :], (((0,), (0,)), ((), ())),
                    preferred_element_type=jnp.float32,
                )
            return carry

        lax.fori_loop(0, (count + GROUP - 1) // GROUP, add_group, 0)

        def store(tile, carry):
            stage[c, tile] = total[tile].astype(stage.dtype)
            if c < chunks - 1:
                total[tile] = jnp.zeros((size, width), jnp.float32)
            return carry

        whole, *pieces = outs[3 * c:3 * c + 3]
        depth = pieces[0].shape[0]
        parts = tiles // depth
        first = 1 + chunks + (parts + 2) * c
        for i in range(parts):
            at = pl.ds(i * depth, depth)
            lax.fori_loop(i * depth, (i + 1) * depth, store, 0)
            leaving.append(pltpu.make_async_copy(stage.at[c, at], whole.at[at], sems.at[first + i]))
            leaving[-1].start()
        for i, ref in enumerate(pieces):
            at = pl.ds(send_ref[2 * c + i] * depth, depth)
            leaving.append(pltpu.make_async_copy(stage.at[c, at], ref, sems.at[first + parts + i]))
            leaving[-1].start()
    for copy in leaving:
        copy.wait()


def tile_sum(panel, columns, width, blocks, row_ids, col_ids, used_count, col_tiles, send):
    slots, size, _ = blocks.shape
    depth = panel.shape[0]
    chunks = len(columns)
    piece = col_tiles // lax.axis_size("z")
    hbm = pl.BlockSpec(memory_space=pl.ANY)
    outs = pl.pallas_call(
        functools.partial(tile_kernel, columns),
        out_shape=[jax.ShapeDtypeStruct((n, size, width), jnp.bfloat16) for n in (col_tiles, piece, piece)] * chunks,
        in_specs=[pl.BlockSpec(memory_space=pltpu.SMEM)] * 4 + [hbm] * 2,
        out_specs=[hbm] * (3 * chunks),
        scratch_shapes=[
            pltpu.VMEM((col_tiles + 1, size, width), jnp.float32),
            pltpu.VMEM(blocks.shape, jnp.bfloat16),
            pltpu.VMEM((chunks, depth, width), jnp.bfloat16),
            pltpu.VMEM((chunks, col_tiles, size, width), jnp.bfloat16),
            pltpu.SemaphoreType.DMA((1 + chunks + (col_tiles // piece + 2) * chunks,)),
        ],
        compiler_params=pltpu.CompilerParams(vmem_limit_bytes=56 * 2**20),
        cost_estimate=pl.CostEstimate(
            flops=2 * slots * size * size * width * chunks,
            bytes_accessed=2 * (blocks.size + depth * width * chunks + col_tiles * size * width * chunks),
            transcendentals=0,
        ),
    )(used_count, send, row_ids, col_ids, blocks, panel)
    return [outs[3 * c:3 * c + 3] for c in range(chunks)]


def behind(value, others):
    return lax.optimization_barrier((value, others))[0]


def shift(value, axis, way):
    size = lax.axis_size(axis)
    return lax.ppermute(value, axis, [(i, (i + way) % size) for i in range(size)])


def row_chains(partial, pieces, ways):
    size = lax.axis_size("z")
    here = lax.axis_index("z")
    arrived = []
    sent = [[] for _ in range(size // 2)]
    for moving, (way, hops) in zip(pieces, ways):
        for hop in range(hops):
            sent[hop].append(moving)
            moving = shift(moving, "z", way)
            left = hops - 1 - hop
            if left:
                place = jnp.bitwise_and(here + way * left, size - 1)
                own = lax.dynamic_index_in_dim(partial, place, 0, keepdims=False)
                moving = (moving.astype(jnp.float32) + own.astype(jnp.float32)).astype(jnp.bfloat16)
        arrived.append(moving)
    return arrived, sent


def row_sum(partials, arrived):
    here = lax.axis_index("z")
    half = lax.axis_index("yh")

    def total(which):
        sums = []
        for partial, terms in zip(partials, arrived):
            width = partial.shape[-1]
            own = partial.reshape(2 * partial.shape[0], -1, width)
            parts = [lax.dynamic_index_in_dim(own, 2 * here + which, 0, keepdims=False)]
            parts += [lax.dynamic_index_in_dim(t.reshape(2, -1, width), which, 0, keepdims=False) for t in terms]
            sums.append(sum(p.astype(jnp.float32) for p in parts))
        return jnp.concatenate(sums, axis=1)

    other = shift(total(1 - half).astype(jnp.bfloat16), "yh", 1)
    return (total(half) + other.astype(jnp.float32)).astype(jnp.bfloat16)


def gather_features(turned, reach):
    found = []
    for start in (turned, shift(turned, "yh", 1)):
        near = {0: start}
        for k in range(1, reach + 1):
            near[k], near[-k] = shift(near[k - 1], "z", -1), shift(near[1 - k], "z", 1)
        found.append(near)
    return found


def term_kernel(chunks, reach, place_ref, *refs):
    partials, refs = refs[:chunks], refs[chunks:]
    passing, refs = refs[:2 * chunks], refs[2 * chunks:]
    features, (out_ref, total, left, nodes, sems) = refs[:-5], refs[-5:]
    z, yh, first = place_ref[0], place_ref[1], place_ref[2]
    rows = out_ref.shape[0]
    count = 2 * reach + 1
    depth = features[0].shape[1]
    width = nodes.shape[2]
    groups = []
    used = 0
    for i in range(count):
        group = []
        for h in range(2):
            b = 2 * i + h
            at = slice(b * depth, (b + 1) * depth)
            source = features[h * count + i].at[pl.ds(pl.multiple_of(first * rows, rows), rows), :]
            group.append(pltpu.make_async_copy(source, left.at[:, at], sems.at[used]))
            used += 1
            half = pl.ds(pl.multiple_of(jnp.bitwise_xor(yh, h) * depth, depth), depth)
            for c in range(chunks):
                if abs(i - reach) == reach:
                    source = passing[2 * c + (i > reach)].at[half, :]
                else:
                    source = partials[c].at[jnp.bitwise_and(z + (i - reach), partials[c].shape[0] - 1), half, :]
                group.append(pltpu.make_async_copy(source, nodes.at[c, at, :], sems.at[used]))
                used += 1
        groups.append(group)
    for group in groups:
        for copy in group:
            copy.start()
    steps = [(0, 1), (1, 3), (3, count)]
    for step, (low, high) in enumerate(steps):
        for group in groups[low:high]:
            for copy in group:
                copy.wait()
        inner = slice(low * 2 * depth, high * 2 * depth)

        for c in range(chunks):
            columns = slice(c * width, (c + 1) * width)
            product = jnp.dot(left[:, inner], nodes[c, inner, :], preferred_element_type=jnp.float32)
            if step:
                product = total[:, columns] + product
            if step < len(steps) - 1:
                total[:, columns] = product
            else:
                out_ref[:, columns] = product.astype(out_ref.dtype)


def weight_terms(features, partials, passing, reach, place):
    distances = list(range(-reach, reach + 1))
    features = [near[k] for near in features for k in distances]
    height, depth = features[0].shape
    width = partials[0].shape[2]
    chunks = len(partials)
    blocks = len(features)
    operands = list(partials) + [p for pair in passing for p in pair] + features
    return pl.pallas_call(
        functools.partial(term_kernel, chunks, reach),
        out_shape=jax.ShapeDtypeStruct((height // 2, chunks * width), jnp.bfloat16),
        in_specs=[pl.BlockSpec(memory_space=pltpu.SMEM)] + [pl.BlockSpec(memory_space=pl.ANY)] * len(operands),
        out_specs=pl.BlockSpec(memory_space=pltpu.VMEM),
        scratch_shapes=[
            pltpu.VMEM((height // 2, chunks * width), jnp.float32),
            pltpu.VMEM((height // 2, blocks * depth), jnp.bfloat16),
            pltpu.VMEM((chunks, blocks * depth, width), jnp.bfloat16),
            pltpu.SemaphoreType.DMA(((1 + chunks) * blocks,)),
        ],
        compiler_params=pltpu.CompilerParams(vmem_limit_bytes=56 * 2**20),
        cost_estimate=pl.CostEstimate(
            flops=height * blocks * depth * chunks * width,
            bytes_accessed=2 * blocks * depth * (height // 2 + chunks * width) + height * chunks * width,
            transcendentals=0,
        ),
    )(place, *operands)


def place_kernel(which_ref, half_ref, *refs):
    out_hbm, stage, sem = refs[-3:]
    rows = stage.shape[0]
    stage[...] = half_ref[...].astype(stage.dtype)
    copy = pltpu.make_async_copy(stage, out_hbm.at[pl.ds(pl.multiple_of(which_ref[0] * rows, rows), rows), :], sem)
    copy.start()
    copy.wait()


def place_half(half, which, whole=()):
    rows, width = half.shape
    whole = [whole] if len(whole) else []
    hbm = pl.BlockSpec(memory_space=pl.ANY)
    return pl.pallas_call(
        place_kernel,
        out_shape=jax.ShapeDtypeStruct((2 * rows, width), jnp.float32),
        in_specs=[pl.BlockSpec(memory_space=pltpu.SMEM), pl.BlockSpec(memory_space=pltpu.VMEM)] + [hbm] * len(whole),
        out_specs=hbm,
        scratch_shapes=[pltpu.VMEM((rows, width), jnp.float32), pltpu.SemaphoreType.DMA],
        input_output_aliases={2: 0} if whole else {},
    )(which.reshape(1), half, *whole)


def sum_everywhere(mine, other, second, third):
    side = lax.axis_size(SIDE)
    depth = lax.axis_size("z")
    core = lax.axis_index("core")
    part = mine.astype(jnp.float32) + shift(other, "core", 1).astype(jnp.float32)
    part = part.astype(jnp.bfloat16).reshape(side, -1, part.shape[-1])
    part = lax.all_to_all(part, SIDE, 0, 0, tiled=True)
    part = jnp.sum(part.astype(jnp.float32), axis=0).astype(jnp.bfloat16)
    part = behind(part, second)
    part = lax.all_to_all(jnp.broadcast_to(part[None], (depth,) + part.shape), "z", 0, 0, tiled=True)
    part = jnp.sum(part.astype(jnp.float32), axis=0).astype(jnp.bfloat16)
    part = behind(part, third)
    half = lax.all_to_all(jnp.broadcast_to(part[None], (side,) + part.shape), SIDE, 0, 0, tiled=True)
    half = half.reshape(-1, half.shape[-1])
    return place_half(shift(half, "core", 1), 1 - core, place_half(half, core))


def per_device(grad_out, preact, features, weight, tile_values, tile_row, tile_col, tile_count):
    size = tile_values.shape[-1]
    width = grad_out.shape[-1] // CHUNKS
    col_tiles = features.shape[1] * lax.axis_size(ROW) // size
    tiles = (tile_values[0, 0], tile_row[0, 0], tile_col[0, 0], tile_count[0], col_tiles)
    z, depth = lax.axis_index("z"), lax.axis_size("z")

    panel = lax.all_gather(silu_grad(grad_out[0], preact[0]), COL, axis=0, tiled=True)
    near = gather_features(features[0].T, REACH)
    ways = (((1, 4), (-1, 3)), ((1, 3), (-1, 4)))
    before = [near_by[k] for near_by in near for k in (REACH, -REACH)]
    partials = []
    passing = []
    arrived = []
    sent = [[] for _ in range(depth // 2)]
    send = jnp.stack([jnp.bitwise_and(z + way * hops, depth - 1) for pair in ways for way, hops in pair])
    columns = tuple(c * width for c in range(CHUNKS))
    chunks = tile_sum(panel, columns, width, *tiles, behind(send, before))
    for (whole, *pieces), pair in zip(chunks, ways):
        partials.append(whole.reshape(depth, -1, width))
        ends, moves = row_chains(partials[-1], [p.reshape(-1, width) for p in pieces], pair)
        arrived.append(ends)
        for hop, sums in enumerate(moves):
            sent[hop] += sums
        far = {way: moves[hops - REACH][i] for i, (way, hops) in enumerate(pair)}
        passing.append((far[-1], far[1]))
    core = lax.axis_index("core")
    theirs, ours = [jnp.stack([z, lax.axis_index("yh"), half]) for half in (1 - core, core)]
    theirs = weight_terms(near, partials, passing, REACH, theirs)
    ours = weight_terms(near, partials, passing, REACH, behind(ours, theirs))
    mixed = row_sum(partials, arrived)
    grad_weight = sum_everywhere(ours, theirs, sent[3], mixed)
    grad_in = lax.dot_general(
        mixed, weight, (((1,), (1,)), ((), ())), preferred_element_type=jnp.float32
    )
    return (grad_in.astype(jnp.bfloat16)[None], grad_weight)


def solution(mesh):
    devices = mesh.devices.reshape(8, 2, 4, 2, 2)
    fine = Mesh(devices, ROW + COL)
    return jax.shard_map(
        per_device,
        mesh=fine,
        in_specs=(
            P(ROW, COL, None),
            P(ROW, COL, None),
            P(COL, ROW, None),
            P(),
            P(ROW, COL, None, None, None),
            P(ROW, COL, None),
            P(ROW, COL, None),
            P(ROW, COL),
        ),
        out_specs=(P(COL, ROW, None), P()),
        check_vma=False,
    )
```
